256 devices in a mesh: inst: 16 (over z, core), tp: 16 (over x, y).
Axes of the slice: x: 4, y: 4, z: 8, core: 2. Of those that a mesh axis runs over, the one named last changes fastest.
Arguments:
- hidden_in: bfloat16 [2, 2048, 8192], P(None, 'inst', 'tp'), may hold values from -128 to 128
- norm_gain: bfloat16 [8192], P('tp'), may hold values from 0.5 to 1.5
- query_weight: bfloat16 [8192, 4096], P(None, 'tp'), may hold values from -0.0625 to 0.0625
- w_key: bfloat16 [8192, 512], P(None, 'tp'), may hold values from -0.0625 to 0.0625
- value_weight: bfloat16 [8192, 512], P(None, 'tp'), may hold values from -0.0625 to 0.0625
- w_output: bfloat16 [4096, 8192], P('tp'), may hold values from -0.25 to 0.25
- paired_down_matrices: bfloat16 [128, 8192, 128], P('inst', 'tp'), may hold values from -0.0625 to 0.0625
- query_up_matrices: bfloat16 [128, 64, 4096], P('inst', None, 'tp'), may hold values from -0.75 to 0.75
- value_up_matrices: bfloat16 [128, 64, 512], P('inst', None, 'tp'), may hold values from -0.75 to 0.75
- output_down_matrices: bfloat16 [128, 64, 4096], P('inst', None, 'tp'), may hold values from -0.25 to 0.25
- output_up_matrices: bfloat16 [128, 64, 8192], P('inst', None, 'tp'), may hold values from -0.75 to 0.75
- key_cache: bfloat16 [2048, 64, 512], P(('inst', 'tp')), may hold values from -160 to 160
- value_cache: bfloat16 [2048, 64, 512], P(('inst', 'tp')), may hold values from -6 to 6
- cache_lengths: int32 [2048], P(('inst', 'tp')), may hold values from 1 to 64, as said below
- row_adapter: int32 [2048], P('inst'), may hold values from 0 to 127, as said below
- old_slot: int32 [128], replicated, may hold values from 0 to 127, as said below
- new_slot: int32 [128], replicated, may hold values from 0 to 127, as said below
Outputs:
- block_out: bfloat16 [2, 2048, 8192], P(None, 'inst', 'tp')
The draws below stay inside these ranges and needn't reach their ends.
Inputs may be any that keep to these rules, and one draw needn't show every extreme that they name: Each value appears once: adapter a is stored in slot old_slot[a] of the adapter arrays, and slot k belongs to instance k // 8. Each value appears once: after migration adapter a sits in slot new_slot[a], on instance new_slot[a] // 8. No instance sends more than one adapter to any one instance, itself included. `row_adapter`: the rows of instance i (rows i * 128 to (i + 1) * 128 - 1) name only adapters that new_slot places on instance i, each of them at least once; the rows of one adapter are contiguous, in increasing order of its new slot. `cache_lengths`: among the rows of each instance at least one has exactly 64.
All inputs are finite; a program needn't handle non-finite values.
Results may differ from the reference program's by a relative error of at most 0.019.
The reference program's roundings to bfloat16 on the way count: a program that leaves them out, or rounds other values in their place, can miss the bound.
Values may be sent and summed in bfloat16 or wider, within the bound.
A program may use at most 128 MiB of HBM per device.

```python
import math
import jax
import jax.numpy as jnp
from jax import lax

D = 8192
HEADS = 32
KV_HEADS = 4
HD = 128
ADAPTER_RANK = 64
ADP_INST = 8
ROWS = 128
LMAX = 64
INSTANCES = 16
ADAPTERS = 128
ALL_ROWS = 2048
QW = 4096
KVW = 512


def assignment(base_key):
    key_old, key_order, key_offset, key_rotation = jax.random.split(base_key, 4)
    old_table = jax.random.permutation(key_old, ADAPTERS).astype(jnp.int32)
    instance_order = jax.random.permutation(key_order, INSTANCES).astype(jnp.int32)
    offsets = jax.random.permutation(key_offset, INSTANCES)[:ADP_INST].astype(jnp.int32)
    rotation = jax.random.randint(key_rotation, (INSTANCES,), 0, ADP_INST, dtype=jnp.int32)
    rank_of = jnp.zeros((INSTANCES,), jnp.int32).at[instance_order].set(jnp.arange(INSTANCES, dtype=jnp.int32))
    slot_ids = jnp.arange(ADAPTERS, dtype=jnp.int32)
    source = slot_ids // ADP_INST
    within = slot_ids % ADP_INST
    target = instance_order[(rank_of[source] + offsets[within]) % INSTANCES]
    position = (within + rotation[target]) % ADP_INST
    slot_new = target * ADP_INST + position
    new_table = slot_new[old_table]
    return (old_table, new_table)


def draw_old_slot(key, part):
    old_table, new_table = assignment(key)
    return old_table


def draw_new_slot(key, part):
    old_table, new_table = assignment(key)
    return new_table


def draw_row_adapter(key, part):
    old_table, new_table = assignment(key)
    key = jax.random.fold_in(key, 3)
    holder = jnp.zeros((ADAPTERS,), jnp.int32).at[new_table].set(jnp.arange(ADAPTERS, dtype=jnp.int32))

    def one_instance(instance_key, instance_id):
        boundaries = jax.random.permutation(instance_key, ROWS - 1)[:ADP_INST - 1].astype(jnp.int32) + 1
        row_ids = jnp.arange(ROWS, dtype=jnp.int32)
        segment = jnp.sum((boundaries[None, :] <= row_ids[:, None]).astype(jnp.int32), axis=1)
        return holder[instance_id * ADP_INST + segment]
    instance_keys = jax.random.split(key, INSTANCES)
    return jax.vmap(one_instance)(instance_keys, jnp.arange(INSTANCES, dtype=jnp.int32)).reshape(ALL_ROWS)


def draw_cache_lengths(key, part):
    key = jax.random.fold_in(key, 4)
    key_length, key_longest = jax.random.split(key)
    lengths = jax.random.randint(key_length, (INSTANCES, ROWS), 1, LMAX + 1, dtype=jnp.int32)
    longest = jax.random.randint(key_longest, (INSTANCES,), 0, ROWS, dtype=jnp.int32)
    lengths = jnp.where(jnp.arange(ROWS, dtype=jnp.int32)[None, :] == longest[:, None], LMAX, lengths)
    return lengths.reshape(ALL_ROWS)


def draw_hidden_in(key, part):
    key = jax.random.fold_in(key, 5)
    key_column, key_row, key_noise = jax.random.split(key, 3)
    rising = 3.0 ** (jnp.arange(D, dtype=jnp.float32) / D)
    column_scale = rising * jnp.exp(jax.random.uniform(key_column, (D,), minval=-1.15, maxval=1.15))
    row_scale = jnp.exp(jax.random.uniform(key_row, (2, ALL_ROWS, 1), minval=-1.15, maxval=1.15))
    noise_part = jnp.clip(jax.random.normal(key_noise, (2, ALL_ROWS, D)), -4.0, 4.0)
    return (noise_part * row_scale * column_scale[None, None, :]).astype(jnp.bfloat16)


def draw_key_cache(key, part):
    key = jax.random.fold_in(key, 6)
    key_values = jax.random.fold_in(key, 0)
    return jnp.clip(jax.random.normal(key_values, (ALL_ROWS, LMAX, KVW)), -4.0, 4.0).astype(jnp.bfloat16)


def level_of(stream_key, extent, shards, least, largest):
    factor_of, own = 1.0, jax.random.fold_in(stream_key, 6)
    for dim, blocks in shards:
        heights = jnp.exp(jax.random.uniform(jax.random.fold_in(own, dim), (blocks,), jnp.float32, least / len(shards), largest / len(shards)))
        factor_of = factor_of * jnp.repeat(heights, extent[dim] // blocks).reshape([-1 if axis == dim else 1 for axis in range(len(extent))])
    return factor_of


def bell_draw(key, shape, scale, most, cuts=(), held_as=jnp.bfloat16):
    loudness = level_of(key, shape, cuts, -0.22, 0.18) if cuts else 1.0
    values = jax.random.normal(key, shape, jnp.float32) * scale * loudness
    return jnp.minimum(jnp.maximum(values, -most), most).astype(held_as)


def setup_inputs(seed: int = 0) -> dict:
    seeds = jax.random.split(jax.random.key(seed), 18)
    hidden_in = draw_hidden_in(jax.random.fold_in(seeds[17], 71), 0)
    norm_gain = jnp.clip(1.0 + 0.1 * jax.random.normal(seeds[1], (D,), jnp.float32), 0.5, 1.5).astype(jnp.bfloat16)
    query_weight = bell_draw(seeds[2], (D, QW), D ** -0.5, 0.0625, ((1, 16),))
    w_key = bell_draw(seeds[3], (D, KVW), D ** -0.5, 0.0625, ((1, 16),))
    value_weight = bell_draw(seeds[4], (D, KVW), D ** -0.5, 0.0625, ((1, 16),))
    w_output = bell_draw(seeds[5], (QW, D), (4 * HD) ** -0.5, 0.25, ((0, 16),))
    paired_down_matrices = bell_draw(seeds[6], (ADAPTERS, D, 2 * ADAPTER_RANK), D ** -0.5, 0.0625, ((0, 16), (1, 16)))
    query_up_matrices = bell_draw(seeds[7], (ADAPTERS, ADAPTER_RANK, QW), ADAPTER_RANK ** -0.5, 0.75, ((0, 16), (2, 16)))
    value_up_matrices = bell_draw(seeds[8], (ADAPTERS, ADAPTER_RANK, KVW), ADAPTER_RANK ** -0.5, 0.75, ((0, 16), (2, 16)))
    output_down_matrices = bell_draw(seeds[9], (ADAPTERS, ADAPTER_RANK, QW), (4 * HD) ** -0.5, 0.25, ((0, 16), (2, 16)))
    output_up_matrices = bell_draw(seeds[10], (ADAPTERS, ADAPTER_RANK, D), ADAPTER_RANK ** -0.5, 0.75, ((0, 16), (2, 16)))
    key_cache = draw_key_cache(jax.random.fold_in(seeds[17], 71), 0)
    value_cache = bell_draw(seeds[12], (ALL_ROWS, LMAX, KVW), 1.0, 6.0, ((0, 256),))
    cache_lengths = draw_cache_lengths(jax.random.fold_in(seeds[17], 71), 0)
    row_adapter = draw_row_adapter(jax.random.fold_in(seeds[17], 71), 0)
    old_slot = draw_old_slot(jax.random.fold_in(seeds[17], 71), 0)
    new_slot = draw_new_slot(jax.random.fold_in(seeds[17], 71), 0)
    return {"hidden_in": hidden_in, "norm_gain": norm_gain, "query_weight": query_weight, "w_key": w_key, "value_weight": value_weight, "w_output": w_output, "paired_down_matrices": paired_down_matrices, "query_up_matrices": query_up_matrices, "value_up_matrices": value_up_matrices, "output_down_matrices": output_down_matrices, "output_up_matrices": output_up_matrices, "key_cache": key_cache, "value_cache": value_cache, "cache_lengths": cache_lengths, "row_adapter": row_adapter, "old_slot": old_slot, "new_slot": new_slot}


ADAPTER_SCALING = 0.5
NORM_EPS = 1e-05
ROPE_BASE = 500000.0

def rounded_hidden(values):
    return lax.optimization_barrier(values.astype(jnp.bfloat16))

def rotary(vectors, positions):
    half_width = vectors.shape[-1] // 2
    frequency = ROPE_BASE ** (-jnp.arange(half_width, dtype=jnp.float32) / half_width)
    angles = positions[:, None, None] * frequency[None, None, :]
    cosine = jnp.cos(angles)
    sine_part = jnp.sin(angles)
    first_half = vectors[..., :half_width]
    second_half = vectors[..., half_width:]
    return jnp.concatenate([first_half * cosine - second_half * sine_part, second_half * cosine + first_half * sine_part], axis=-1)

def attend(query_vectors, fresh_keys, fresh_values, key_rows, value_rows, lengths):
    row_count = query_vectors.shape[0]
    group_size = HEADS // KV_HEADS
    grouped = query_vectors.astype(jnp.float32).reshape(row_count, KV_HEADS, group_size, HD)
    cached_keys = key_rows.astype(jnp.float32).reshape(row_count, LMAX, KV_HEADS, HD)
    cached_values = value_rows.astype(jnp.float32).reshape(row_count, LMAX, KV_HEADS, HD)
    score_scale = 1.0 / math.sqrt(HD)
    cache_scores = jnp.einsum('rgqd,rlgd->rgql', grouped, cached_keys) * score_scale
    live_keys = jnp.arange(LMAX, dtype=jnp.int32)[None, :] < lengths[:, None]
    cache_scores = jnp.where(live_keys[:, None, None, :], cache_scores, -jnp.inf)
    new_keys = jnp.stack(fresh_keys, axis=1).astype(jnp.float32)
    new_values = jnp.stack(fresh_values, axis=1).astype(jnp.float32)
    fresh_scores = jnp.einsum('rgqd,rngd->rgqn', grouped, new_keys) * score_scale
    scores = jnp.concatenate([cache_scores, fresh_scores], axis=3)
    row_top = lax.optimization_barrier(jnp.max(scores, axis=3, keepdims=True))
    powers = jnp.exp(scores - row_top)
    weights = rounded_hidden(powers / lax.optimization_barrier(jnp.sum(powers, axis=3, keepdims=True))).astype(jnp.float32)
    mixture = jnp.einsum('rgql,rlgd->rgqd', weights[..., :LMAX], cached_values)
    mixture = mixture + jnp.einsum('rgqn,rngd->rgqd', weights[..., LMAX:], new_values)
    return mixture.reshape(row_count, HEADS * HD)

def reference(hidden_in, norm_gain, query_weight, w_key, value_weight, w_output, paired_down_matrices, query_up_matrices, value_up_matrices, output_down_matrices, output_up_matrices, key_cache, value_cache, cache_lengths, row_adapter, old_slot, new_slot):
    adapter_ids = jnp.arange(ADAPTERS, dtype=jnp.int32)
    holder = jnp.zeros((ADAPTERS,), jnp.int32).at[new_slot].set(adapter_ids)
    source_slot = old_slot[holder].reshape(INSTANCES, ADP_INST)
    instance_ids = jnp.arange(INSTANCES, dtype=jnp.int32)
    row_local = new_slot[row_adapter].reshape(INSTANCES, ROWS) - ADP_INST * instance_ids[:, None]
    hidden_split = jnp.transpose(hidden_in.reshape(2, INSTANCES, ROWS, D), (1, 0, 2, 3))
    gain_values = norm_gain.astype(jnp.float32)
    current_row_index = jnp.arange(ROWS, dtype=jnp.int32)

    def one_instance(packed):
        hidden, source_slot_list, resident_slot_index, key_rows, value_rows, lengths = packed
        row_down_matrices = paired_down_matrices[source_slot_list].astype(jnp.float32)
        row_query_up = query_up_matrices[source_slot_list].astype(jnp.float32)
        row_value_up = value_up_matrices[source_slot_list].astype(jnp.float32)
        row_output_down = output_down_matrices[source_slot_list].astype(jnp.float32)
        row_output_up = output_up_matrices[source_slot_list].astype(jnp.float32)
        step_outputs = []
        fresh_keys = []
        fresh_values = []
        for step_index in range(2):
            values32 = hidden[step_index].astype(jnp.float32)
            mean_square = lax.optimization_barrier(jnp.mean(values32 * values32, axis=1, keepdims=True))
            normalized_hidden = rounded_hidden(values32 * lax.rsqrt(mean_square + NORM_EPS) * gain_values[None, :])
            rank_projection_total = jnp.einsum('bs,hsi->hbi', normalized_hidden.astype(jnp.float32), row_down_matrices)
            rank_projection_input = rounded_hidden(rank_projection_total[resident_slot_index, current_row_index]).astype(jnp.float32)
            query_delta = jnp.einsum('za,dao->dzo', rank_projection_input[:, :ADAPTER_RANK], row_query_up)[resident_slot_index, current_row_index]
            value_delta = jnp.einsum('za,dao->dzo', rank_projection_input[:, ADAPTER_RANK:], row_value_up)[resident_slot_index, current_row_index]
            query_vectors = rounded_hidden(jnp.dot(normalized_hidden, query_weight, preferred_element_type=jnp.float32) + ADAPTER_SCALING * query_delta)
            key_fresh = rounded_hidden(jnp.dot(normalized_hidden, w_key, preferred_element_type=jnp.float32))
            value_current_step = rounded_hidden(jnp.dot(normalized_hidden, value_weight, preferred_element_type=jnp.float32) + ADAPTER_SCALING * value_delta)
            positions = (lengths + step_index).astype(jnp.float32)
            query_rot = rounded_hidden(rotary(query_vectors.astype(jnp.float32).reshape(ROWS, HEADS, HD), positions))
            key_rot = rounded_hidden(rotary(key_fresh.astype(jnp.float32).reshape(ROWS, KV_HEADS, HD), positions))
            fresh_keys.append(key_rot)
            fresh_values.append(value_current_step.reshape(ROWS, KV_HEADS, HD))
            attention_result = rounded_hidden(attend(query_rot, fresh_keys, fresh_values, key_rows, value_rows, lengths))
            output_total = jnp.einsum('uv,xlv->xul', attention_result.astype(jnp.float32), row_output_down)
            output_rank_vectors = rounded_hidden(output_total[resident_slot_index, current_row_index]).astype(jnp.float32)
            output_delta = jnp.einsum('us,gsy->guy', output_rank_vectors, row_output_up)[resident_slot_index, current_row_index]
            base_projection_output = jnp.dot(attention_result, w_output, preferred_element_type=jnp.float32)
            step_outputs.append((base_projection_output + ADAPTER_SCALING * output_delta).astype(jnp.bfloat16))
        return jnp.stack(step_outputs, axis=0)
    result = lax.map(one_instance, (hidden_split, source_slot, row_local, key_cache.reshape(INSTANCES, ROWS, LMAX, KVW), value_cache.reshape(INSTANCES, ROWS, LMAX, KVW), cache_lengths.reshape(INSTANCES, ROWS)))
    return jnp.transpose(result, (1, 0, 2, 3)).reshape(2, ALL_ROWS, D)
```

```python
import functools
import math

import jax
import jax.numpy as jnp
from jax import lax
from jax.experimental import pallas as pl
from jax.experimental.pallas import tpu as pltpu
from jax.sharding import PartitionSpec as P

MESH = pl.DeviceIdType.MESH
F32, BF16 = jnp.float32, jnp.bfloat16

NT = 16
NI = 16
SIDE = 4
D = 8192
SH = 512
ROWS = 128
R2 = 256
OWN = 16
HEADS = 32
HD = 128
SLOTS = 8
LMAX = 64
LPAD = 80
ADAPTER_SCALING = 0.5
NORM_EPS = 1e-05
ROPE_BASE = 500000.0

SCRATCH = dict(
    hidv=((2, ROWS, SH), BF16),
    ag=((NT, R2, SH), BF16),
    wqv=((D, 256), BF16),
    wkv=((256, D), BF16),
    wof=((NT, 2, 128, SH), BF16),
    dnv=((SLOTS, SH, 128), BF16),
    quv=((SLOTS, 64, 256), BF16),
    vuv=((SLOTS, 32, 64), BF16),
    odv=((SLOTS, 64, 256), BF16),
    ouv=((SLOTS, 64, SH), BF16),
    dns=((NI, SH, 128), BF16),
    qus=((NI, 64, 256), BF16),
    vus=((NI, 32, 128), BF16),
    ods=((NI, 64, 256), BF16),
    ous=((NI, 64, SH), BF16),
    dnr=((NI, SH, 128), BF16),
    qur=((NI, 64, 256), BF16),
    vur=((NI, 32, 128), BF16),
    odr=((NI, 64, 256), BF16),
    our=((NI, 64, SH), BF16),
    qcat=((SLOTS * 128, 256), BF16),
    vcat=((128, SLOTS * 128), BF16),
    oucat=((SLOTS * 128, SH), BF16),
    rall=((R2, SLOTS * 128), BF16),
    rall2=((R2, SLOTS * 128), BF16),
    kext=((8, LPAD, 512), BF16),
    vext=((8, LPAD, 512), BF16),
    ssb=((NT, 8, 128), F32),
    rs1s=((NT, OWN, 128), F32),
    rs1r=((NT, OWN, 128), F32),
    rk1=((NT, OWN, 128), BF16),
    rs2s=((NT, OWN, 128), F32),
    rs2r=((NT, OWN, 128), F32),
    rk2=((NT, OWN, 128), BF16),
    qacc=((R2, 256), F32),
    kvacc=((R2, 256), F32),
    qkvs=((NT, OWN, 512), BF16),
    qkvr=((NT, OWN, 512), BF16),
    q2=((OWN * HEADS, HD), F32),
    o2=((OWN * HEADS, HD), F32),
    ag2=((NT, OWN, HEADS * HD), BF16),
    attd=((NT, OWN, 256), BF16),
    oacc=((R2, SH), F32),
)
SEMS = dict(
    ld=(16,),
    ss_s=(NT,), ss_r=(NT,),
    ag_s=(2, 20), ag_r=(2, NT, 2),
    z_s=(5, NI), z_r=(5, NI),
    wo_s=(NT,), wo_r=(NT,), sib_s=(1,), sib_r=(1,),
    rs1_s=(NT,), rs1_r=(NT,), rk1_s=(NT,), rk1_r=(NT,),
    qkv_s=(NT,), qkv_r=(NT,),
    ag2_s=(2, 20), ag2_r=(2, NT, 2),
    at_s=(NT,), at_r=(NT,),
    rs2_s=(NT,), rs2_r=(NT,), rk2_s=(NT,), rk2_r=(NT,),
)
INPUTS = (
    "tabs", "lens", "gain", "rmask", "hid", "wq", "wk", "wv", "wo",
    "dn", "qu", "vu", "od", "ou", "kc", "vc",
)


class Refs:
    pass


def dot(a, b):
    return lax.dot_general(a, b, (((1,), (0,)), ((), ())), preferred_element_type=F32)


def dot_nt(a, b):
    return lax.dot_general(a, b, (((1,), (1,)), ((), ())), preferred_element_type=F32)


def remote(src, dst, ssem, rsem, **where):
    return pltpu.make_async_remote_copy(
        src_ref=src, dst_ref=dst, send_sem=ssem, recv_sem=rsem, device_id=where, device_id_type=MESH
    )


def loop(lo, hi, body):
    lax.fori_loop(lo, hi, lambda k, c: (body(k), c)[1], 0)


def peers(me, n, body):
    loop(1, n, lambda k: body(lax.rem(me + k, n)))


def mesh_gather(x, y, ref_of, ssem, rsem):
    def at(p, da, db):
        ax, ay = (da, db) if p == 0 else (db, da)
        return lax.rem(x + ax + SIDE, SIDE) * SIDE + lax.rem(y + ay + SIDE, SIDE)

    count = [0, 0]
    sent = []

    def copy(p, da, db, half, to, idx):
        block = at(p, da, db)
        ref = ref_of(block, p, half)
        return remote(
            ref, ref, ssem.at[p, idx], rsem.at[p, block, half or 0], tp=at(p, *to)
        )

    def send(p, da, db, half, to):
        c = copy(p, da, db, half, to, count[p])
        count[p] += 1
        c.start()
        sent.append(c)

    def wait(p, da, db, half=None):
        copy(p, da, db, half, (1, 0), 0).wait_recv()

    def start():
        for p in range(2):
            for to in ((1, 0), (-1, 0), (0, 1), (0, -1)):
                send(p, 0, 0, None, to)

    def along_b(p, da):
        send(p, da, 0, None, (0, 1))
        send(p, da, 0, None, (0, -1))

    def s1():
        for p in range(2):
            wait(p, -1, 0)
            send(p, -1, 0, 0, (1, 0))
            along_b(p, -1)
        for p in range(2):
            wait(p, 1, 0)
            send(p, 1, 0, 1, (-1, 0))
            along_b(p, 1)

    def s2():
        for p in range(2):
            wait(p, 0, -1)
            send(p, 0, -1, 0, (0, 1))
            wait(p, 0, 1)
            send(p, 0, 1, 1, (0, -1))

    def s3():
        for p in range(2):
            wait(p, 2, 0, 0)
            wait(p, 2, 0, 1)
            along_b(p, 2)

    def s4():
        for da in (-1, 1):
            for p in range(2):
                wait(p, da, -1)
                send(p, da, -1, 0, (0, 1))
                wait(p, da, 1)
                send(p, da, 1, 1, (0, -1))

    def s5():
        for p in range(2):
            wait(p, 0, 2, 0)
            wait(p, 0, 2, 1)

    def s6():
        for p in range(2):
            wait(p, 2, -1)
            send(p, 2, -1, 0, (0, 1))
            wait(p, 2, 1)
            send(p, 2, 1, 1, (0, -1))

    def s7():
        for da in (-1, 1, 2):
            for p in range(2):
                wait(p, da, 2, 0)
                wait(p, da, 2, 1)

    return start, (s1, s2, s3, s4, s5, s6, s7), sent


def kernel(*args):
    names = list(INPUTS) + ["out"] + list(SCRATCH) + list(SEMS)
    r = Refs()
    for name, ref in zip(names, args, strict=True):
        setattr(r, name, ref)
    i = lax.axis_index("inst")
    t = lax.axis_index("tp")
    x, y = t // SIDE, lax.rem(t, SIDE)
    core = lax.rem(i, 2)
    sibling = i + 1 - 2 * core

    loads = {}

    def load(name, src, dst):
        c = pltpu.make_async_copy(src, dst, r.ld.at[len(loads)])
        c.start()
        loads[name] = c

    load("hid", r.hid, r.hidv)
    for m in ("dn", "qu", "vu", "od", "ou"):
        load(m, getattr(r, m), getattr(r, m + "v"))

    bar = pltpu.get_barrier_semaphore()

    def hello(axis, p):
        pl.semaphore_signal(bar, inc=1, device_id={axis: p}, device_id_type=MESH)

    peers(t, NT, lambda p: hello("tp", p))
    peers(i, NI, lambda p: hello("inst", p))

    eye = lax.broadcasted_iota(jnp.int32, (128, 128), 0) == lax.broadcasted_iota(
        jnp.int32, (128, 128), 1
    )
    loads["hid"].wait()
    parts = []
    for s in range(2):
        h = r.hidv[s].astype(F32)
        column = jnp.sum(h * h, axis=1, keepdims=True)
        parts.append(jnp.sum(jnp.where(eye, column, 0.0), axis=0, keepdims=True))
    r.ssb[t] = jnp.concatenate(parts + [jnp.zeros((6, 128), F32)], axis=0)

    pl.semaphore_wait(bar, NT + NI - 2)

    def ss_copy(src_block, to):
        return remote(
            r.ssb.at[src_block], r.ssb.at[src_block], r.ss_s.at[to], r.ss_r.at[src_block], tp=to
        )

    peers(t, NT, lambda p: ss_copy(t, p).start())

    kinds = ("dn", "qu", "vu", "od", "ou")

    def z_copy(m, block, slot, to):
        st, rc = getattr(r, kinds[m] + "s"), getattr(r, kinds[m] + "r")
        return remote(st.at[block], rc.at[slot], r.z_s.at[m, to], r.z_r.at[m, slot], inst=to)

    def send_kind(m):
        loads[kinds[m]].wait()
        have, st, rc = (getattr(r, kinds[m] + e) for e in "vsr")
        if kinds[m] == "vu":
            st[...] = jnp.zeros_like(st)

        def stage(j):
            block = have[r.tabs[j]]
            if kinds[m] == "vu":
                st[j, :, 0:64] = block
            else:
                st[j] = block

        loop(0, NI, stage)
        peers(i, NI, lambda p: z_copy(m, p, i, p).start())
        rc[i] = st[i]

    send_kind(0)

    peers(t, NT, lambda p: ss_copy(p, p).wait_recv())
    total = jnp.sum(r.ssb[...], axis=0)
    gain = r.gain[...].astype(F32)
    normed = []
    for s in range(2):
        column = jnp.sum(jnp.where(eye, total[s : s + 1, :], 0.0), axis=1, keepdims=True)
        scale = lax.rsqrt(column * (1.0 / D) + NORM_EPS)
        normed.append(r.hidv[s].astype(F32) * scale * gain)
    for p in range(NT):
        r.ag[t, p * OWN : (p + 1) * OWN] = jnp.concatenate(
            [n[8 * p : 8 * p + 8] for n in normed], axis=0
        ).astype(BF16)

    def ag_ref(block, p, half):
        if half is None:
            return r.ag.at[block, pl.ds(p * 128, 128)]
        return r.ag.at[block, pl.ds(p * 128 + half * 64, 64)]

    start, steps, sent1 = mesh_gather(x, y, ag_ref, r.ag_s, r.ag_r)
    start()

    for m in range(1, 5):
        send_kind(m)

    load("wq", r.wq, r.wqv)
    r.wkv[...] = jnp.zeros_like(r.wkv)
    lane0 = pl.multiple_of(32 * lax.rem(t, 4), 32)
    load("wk", r.wk, r.wkv.at[pl.ds(lane0, 32)])
    load("wv", r.wv, r.wkv.at[pl.ds(128 + lane0, 32)])
    load("kc", r.kc, r.kext.at[:, pl.ds(0, LMAX)])
    load("vc", r.vc, r.vext.at[:, pl.ds(0, LMAX)])
    steps[0]()
    steps[1]()
    for ref in (r.qcat, r.vcat, r.oucat, r.qacc, r.kvacc, r.rs2s):
        ref[...] = jnp.zeros_like(ref)
    for step in steps[2:]:
        step()

    def wo_src(p):
        return r.wo.at[pl.ds(core * 128, 128), pl.ds(pl.multiple_of(p * SH, SH), SH)]

    def wo_copy(row, to):
        return remote(wo_src(to), r.wof.at[row, core], r.wo_s.at[to], r.wo_r.at[row], tp=to)

    peers(t, NT, lambda p: wo_copy(t, p).start())
    load("wo", wo_src(t), r.wof.at[t, core])

    for name in ("wq", "wk", "wv"):
        loads[name].wait()

    def project(b):
        cols = pl.ds(pl.multiple_of(b * SH, SH), SH)
        block = r.ag[b]
        r.qacc[...] += dot(block, r.wqv[cols, :])
        r.kvacc[...] += dot_nt(block, r.wkv[:, cols])

    loop(0, NT, project)

    def z_wait(m):
        peers(i, NI, lambda p: z_copy(m, p, p, p).wait_recv())

    def reduce_rows(own, send, recv, gathered, s1, r1, s2, r2):
        def c1(block, slot, to):
            return remote(send.at[block], recv.at[slot], s1.at[to], r1.at[slot], tp=to)

        def c2(slot, to):
            return remote(gathered.at[slot], gathered.at[slot], s2.at[to], r2.at[slot], tp=to)

        peers(t, NT, lambda p: c1(p, t, p).start())
        recv[t] = send[t]
        peers(t, NT, lambda p: c1(p, p, p).wait_recv())
        gathered[t] = jnp.sum(recv[...], axis=0).astype(BF16)
        peers(t, NT, lambda p: c2(t, p).start())
        peers(t, NT, lambda p: c2(p, p).wait_recv())

        def finish():
            peers(t, NT, lambda p: c1(p, p, p).wait_send())
            peers(t, NT, lambda p: c2(p, p).wait_send())

        return gathered[...].reshape(R2, 128).astype(F32), finish

    slot_of_row = r.rmask[...]
    z_wait(0)
    mine = r.ag[t]
    part = jnp.zeros((R2, 128), F32)
    for k in range(SLOTS):
        got = dot(mine, r.dnr[r.tabs[NI + k]])
        part = jnp.where(slot_of_row == k, got, part)
    r.rs1s[...] = part.reshape(NT, OWN, 128)
    rank, finish1 = reduce_rows(
        t, r.rs1s, r.rs1r, r.rk1, r.rs1_s, r.rs1_r, r.rk1_s, r.rk1_r
    )
    rolled = pltpu.roll(rank, 64, 1)
    for k in range(SLOTS):
        cols = slice(k * 128, (k + 1) * 128)
        r.rall[:, cols] = jnp.where(slot_of_row == k, rank, 0.0).astype(BF16)
        r.rall2[:, cols] = jnp.where(slot_of_row == k, rolled, 0.0).astype(BF16)

    z_wait(1)
    z_wait(2)
    for k in range(SLOTS):
        r.qcat[k * 128 : k * 128 + 64] = r.qur[r.tabs[NI + k]]
        r.vcat[pl.ds(lane0, 32), k * 128 : (k + 1) * 128] = r.vur[r.tabs[NI + k]]
    query = r.qacc[...] + ADAPTER_SCALING * dot(r.rall[...], r.qcat[...])
    fresh_value = r.kvacc[:, 128:] + ADAPTER_SCALING * dot_nt(r.rall2[...], r.vcat[...])
    r.qkvs[:, :, 0:256] = query.astype(BF16).reshape(NT, OWN, 256)
    r.qkvs[:, :, 256:384] = r.kvacc[:, :128].astype(BF16).reshape(NT, OWN, 128)
    r.qkvs[:, :, 384:512] = fresh_value.astype(BF16).reshape(NT, OWN, 128)

    def qkv_copy(block, slot, to):
        return remote(r.qkvs.at[block], r.qkvr.at[slot], r.qkv_s.at[to], r.qkv_r.at[slot], tp=to)

    peers(t, NT, lambda p: qkv_copy(p, t, p).start())
    r.qkvr[t] = r.qkvs[t]

    loads["wo"].wait()
    peers(t, NT, lambda p: wo_copy(p, p).wait_recv())
    sib = remote(
        r.wof.at[:, core], r.wof.at[:, core], r.sib_s.at[0], r.sib_r.at[0], inst=sibling
    )
    sib.start()

    row = lax.broadcasted_iota(jnp.int32, (OWN, HD), 0)
    lane = lax.broadcasted_iota(jnp.int32, (OWN, HD), 1)
    step_of_row = row // 8
    positions = step_of_row
    for b in range(8):
        positions = positions + jnp.where(lax.rem(row, 8) == b, r.lens[b], 0)
    freq = jnp.exp(lax.rem(lane, 64).astype(F32) * (-math.log(ROPE_BASE) / 64))
    angle = positions.astype(F32) * freq
    cos2 = jnp.cos(angle)
    sin2 = jnp.sin(angle)
    sin2 = jnp.where(lane < 64, -sin2, sin2)

    def rotate(v):
        return v * cos2 + pltpu.roll(v, 64, 1) * sin2

    peers(t, NT, lambda p: qkv_copy(p, p, p).wait_recv())
    loads["kc"].wait()
    loads["vc"].wait()
    for b in range(NT):
        for h in range(2):
            head = r.qkvr[b, :, h * HD : (h + 1) * HD].astype(F32)
            r.q2[pl.ds(2 * b + h, OWN, stride=HEADS)] = rotate(head)
    for g in range(4):
        cols = slice(g * HD, (g + 1) * HD)
        key = jnp.zeros((OWN, HD), F32)
        val = jnp.zeros((OWN, HD), F32)
        for b in range(4 * g, 4 * g + 4):
            key += r.qkvr[b, :, 256:384].astype(F32)
            val += r.qkvr[b, :, 384:512].astype(F32)
        key = rotate(key)
        for b in range(8):
            for v, ref in ((key, r.kext), (val, r.vext)):
                ref[b, LMAX:LPAD, cols] = jnp.where(
                    row == 0, v[b : b + 1], jnp.where(row == 1, v[8 + b : 9 + b], 0.0)
                ).astype(BF16)
    at_key = lax.broadcasted_iota(jnp.int32, (OWN, LPAD), 1)
    at_step = lax.broadcasted_iota(jnp.int32, (OWN, LPAD), 0) // 8
    for b in range(8):
        live = at_key < jnp.where(at_key < LMAX, r.lens[b], LMAX + 1 + at_step)
        for g in range(4):
            cols = slice(g * HD, (g + 1) * HD)
            q = jnp.concatenate(
                [
                 r.q2[(s * 8 + b) * HEADS + 8 * g : (s * 8 + b) * HEADS + 8 * g + 8]
                 for s in range(2)], axis=0
            ).astype(BF16)
            score = dot_nt(q, r.kext[b, :, cols]) * (1.0 / math.sqrt(HD))
            score = jnp.where(live, score, -jnp.inf)
            power = jnp.exp(score - jnp.max(score, axis=1, keepdims=True))
            weight = (power / jnp.sum(power, axis=1, keepdims=True)).astype(BF16)
            mix = dot(weight, r.vext[b, :, cols])
            for s in range(2):
                lo = (s * 8 + b) * HEADS + 8 * g
                r.o2[lo : lo + 8] = mix[s * 8 : s * 8 + 8]
    for h in range(HEADS):
        r.ag2[t, :, h * HD : (h + 1) * HD] = r.o2[pl.ds(h, OWN, stride=HEADS)].astype(BF16)

    def at_copy(cols_of, slot, to):
        src = r.ag2.at[t, :, pl.ds(pl.multiple_of(cols_of * 256, 256), 256)]
        return remote(src, r.attd.at[slot], r.at_s.at[to], r.at_r.at[slot], tp=to)

    peers(t, NT, lambda p: at_copy(p, t, p).start())

    def ag2_ref(block, p, half):
        if half is None:
            return r.ag2.at[block, :, pl.ds(p * 2048, 2048)]
        return r.ag2.at[block, :, pl.ds(p * 2048 + half * 1024, 1024)]

    start, steps, sent2 = mesh_gather(x, y, ag2_ref, r.ag2_s, r.ag2_r)
    start()
    r.attd[t] = r.ag2[t, :, pl.ds(pl.multiple_of(t * 256, 256), 256)]
    z_wait(3)
    steps[0]()
    steps[1]()
    peers(t, NT, lambda p: at_copy(p, p, p).wait_recv())
    heads = r.attd[...].reshape(R2, 256)
    part = jnp.zeros((R2, 64), F32)
    for k in range(SLOTS):
        got = dot_nt(heads, r.odr[r.tabs[NI + k]])
        part = jnp.where(slot_of_row[:, :64] == k, got, part)
    r.rs2s[:, :, 0:64] = part.reshape(NT, OWN, 64)
    for step in steps[2:4]:
        step()
    rank, finish2 = reduce_rows(
        t, r.rs2s, r.rs2r, r.rk2, r.rs2_s, r.rs2_r, r.rk2_s, r.rk2_r
    )
    for k in range(SLOTS):
        cols = slice(k * 128, (k + 1) * 128)
        r.rall[:, cols] = jnp.where(slot_of_row == k, rank, 0.0).astype(BF16)
    for step in steps[4:]:
        step()

    sib_in = remote(
        r.wof.at[:, 1 - core], r.wof.at[:, 1 - core], r.sib_s.at[0], r.sib_r.at[0], inst=sibling
    )
    sib_in.wait_recv()
    r.oacc[...] = jnp.zeros_like(r.oacc)

    def out_chunk(c):
        lhs = r.ag2[:, :, pl.ds(pl.multiple_of(c * 512, 512), 512)].reshape(R2, 512)
        rhs = r.wof[pl.ds(c * 2, 2)].reshape(512, SH)
        r.oacc[...] += dot(lhs, rhs)

    loop(0, 8, out_chunk)
    z_wait(4)
    for k in range(SLOTS):
        r.oucat[k * 128 : k * 128 + 64] = r.our[r.tabs[NI + k]]
    res = r.oacc[...] + ADAPTER_SCALING * dot(r.rall[...], r.oucat[...])
    for p in range(NT):
        for s in range(2):
            lo = p * OWN + s * 8
            r.oacc[s * ROWS + p * 8 : s * ROWS + p * 8 + 8] = res[lo : lo + 8]
    for s in range(2):
        r.out[s] = r.oacc[s * ROWS : (s + 1) * ROWS].astype(BF16)

    peers(t, NT, lambda p: ss_copy(p, p).wait_send())
    for m in range(5):
        peers(i, NI, lambda p, m=m: z_copy(m, p, p, p).wait_send())
    for c in sent1 + sent2:
        c.wait_send()
    peers(t, NT, lambda p: wo_copy(p, p).wait_send())
    sib.wait_send()
    peers(t, NT, lambda p: qkv_copy(p, p, p).wait_send())
    peers(t, NT, lambda p: at_copy(p, p, p).wait_send())
    finish1()
    finish2()


def local(
    hidden_in,
    norm_gain,
    query_weight,
    w_key,
    value_weight,
    w_output,
    paired_down_matrices,
    query_up_matrices,
    value_up_matrices,
    output_down_matrices,
    output_up_matrices,
    key_cache,
    value_cache,
    cache_lengths,
    row_adapter,
    old_slot,
    new_slot,
):
    i = lax.axis_index("inst")
    ids = jnp.arange(NI, dtype=jnp.int32)
    leaving = (old_slot // SLOTS == i)[None, :] & ((new_slot // SLOTS)[None, :] == ids[:, None])
    source = jnp.sum(jnp.where(leaving, (old_slot % SLOTS)[None, :], 0), axis=1)
    arriving = new_slot[None, :] == (i * SLOTS + jnp.arange(SLOTS, dtype=jnp.int32))[:, None]
    anchor = jnp.sum(jnp.where(arriving, (old_slot // SLOTS)[None, :], 0), axis=1)
    tabs = jnp.concatenate([source, anchor])
    named = row_adapter[:, None] == jnp.arange(new_slot.shape[0], dtype=jnp.int32)[None, :]
    row_slot = jnp.sum(jnp.where(named, (new_slot - i * SLOTS)[None, :], 0), axis=1)
    rmask = jnp.broadcast_to(row_slot.reshape(NT, 1, 8, 1), (NT, 2, 8, 128)).reshape(R2, 128)
    smem = pl.BlockSpec(memory_space=pltpu.SMEM)
    vmem = pl.BlockSpec(memory_space=pltpu.VMEM)
    hbm = pl.BlockSpec(memory_space=pl.ANY)
    return pl.pallas_call(
        kernel,
        out_shape=jax.ShapeDtypeStruct((2, ROWS, SH), BF16),
        in_specs=[smem, smem, vmem, vmem] + [hbm] * 12,
        out_specs=vmem,
        scratch_shapes=[pltpu.VMEM(*s) for s in SCRATCH.values()]
        + [pltpu.SemaphoreType.DMA(s) for s in SEMS.values()],
        compiler_params=pltpu.CompilerParams(
            collective_id=0, has_side_effects=True, vmem_limit_bytes=58 * 2**20
        ),
        name="decode_block",
    )(
        tabs,
        cache_lengths,
        norm_gain.reshape(1, SH),
        rmask,
        hidden_in,
        query_weight,
        w_key.T,
        value_weight.T,
        w_output,
        paired_down_matrices,
        query_up_matrices,
        jnp.swapaxes(value_up_matrices, 1, 2),
        output_down_matrices,
        output_up_matrices,
        key_cache,
        value_cache,
    )


def solution(mesh):
    placed = (
        P(None, "inst", "tp"),
        P("tp"),
        P(None, "tp"),
        P(None, "tp"),
        P(None, "tp"),
        P("tp", None),
        P("inst", "tp", None),
        P("inst", None, "tp"),
        P("inst", None, "tp"),
        P("inst", None, "tp"),
        P("inst", None, "tp"),
        P(("inst", "tp"), None, None),
        P(("inst", "tp"), None, None),
        P(("inst", "tp")),
        P("inst"),
        P(),
        P(),
    )
    return jax.shard_map(
        local, mesh=mesh, in_specs=placed, out_specs=P(None, "inst", "tp"), check_vma=False
    )
```

```python
import functools
import math

import jax
import jax.numpy as jnp
from jax import lax
from jax.experimental import pallas as pl
from jax.experimental.pallas import tpu as pltpu
from jax.sharding import PartitionSpec as P

MESH = pl.DeviceIdType.MESH
F32, BF16 = jnp.float32, jnp.bfloat16

NT = 16
NI = 16
SIDE = 4
D = 8192
SH = 512
ROWS = 128
R2 = 256
OWN = 16
HEADS = 32
HD = 128
SLOTS = 8
LMAX = 64
LPAD = 80
ADAPTER_SCALING = 0.5
NORM_EPS = 1e-05
ROPE_BASE = 500000.0

WO_ORDER = (
    (1, 0), (0, 3), (3, 0), (0, 1), (1, 1), (3, 3), (1, 3), (3, 1),
    (2, 0), (0, 2), (2, 1), (1, 2), (2, 3), (3, 2), (2, 2),
)

SCRATCH = dict(
    tabv=((8, 128), jnp.int32),
    rmask=((R2, 128), F32),
    ag=((NT, 2, ROWS, SH), BF16),
    nrm=((R2, SH), BF16),
    mine=((R2, SH), BF16),
    gains=((NT, 1, SH), F32),
    sc=((8 * 64, LPAD), F32),
    wt=((8 * 64, LPAD), BF16),
    wqv=((D, 256), BF16),
    wkv=((256, D), BF16),
    wof=((NT, 2, 128, SH), BF16),
    dnv=((SLOTS, SH, 128), BF16),
    quv=((SLOTS, 64, 256), BF16),
    vuv=((SLOTS, 32, 64), BF16),
    odv=((SLOTS, 64, 256), BF16),
    ouv=((SLOTS, 64, SH), BF16),
    dns=((NI, SH, 128), BF16),
    qus=((NI, 64, 256), BF16),
    vus=((NI, 32, 128), BF16),
    ods=((NI, 64, 256), BF16),
    ous=((NI, 64, SH), BF16),
    dnr=((NI, SH, 128), BF16),
    qur=((NI, 64, 256), BF16),
    vur=((NI, 32, 128), BF16),
    odr=((NI, 64, 256), BF16),
    our=((NI, 64, SH), BF16),
    qcat=((SLOTS * 128, 256), BF16),
    vcat=((128, SLOTS * 128), BF16),
    oucat=((SLOTS * 128, SH), BF16),
    rall=((R2, SLOTS * 128), BF16),
    rall2=((R2, SLOTS * 128), BF16),
    kext=((8, LPAD, 512), BF16),
    vext=((8, LPAD, 512), BF16),
    ssb=((NT, 8, 128), F32),
    rs1s=((NT, OWN, 128), F32),
    rs1r=((NT, OWN, 128), F32),
    rk1=((NT, OWN, 128), BF16),
    rs2s=((NT, OWN, 128), F32),
    rs2r=((NT, OWN, 128), F32),
    rk2=((NT, OWN, 128), BF16),
    qacc=((R2, 256), F32),
    kvacc=((R2, 256), F32),
    qkvs=((NT, OWN, 512), BF16),
    qkvr=((NT, OWN, 512), BF16),
    q2=((OWN * HEADS, HD), F32),
    o2=((OWN * HEADS, HD), F32),
    ag2=((NT, OWN, HEADS * HD), BF16),
    attd=((NT, OWN, 256), BF16),
    oacc=((R2, SH), F32),
)
SEMS = dict(
    ld=(16,),
    ss_s=(NT,), ss_r=(NT,),
    ag_s=(2, 20), ag_r=(2, NT, 2),
    z_s=(5, NI), z_r=(5, NI),
    wo_s=(NT,), wo_r=(NT,), sib_s=(1,), sib_r=(1,),
    rs1_s=(NT,), rs1_r=(NT,), rk1_s=(NT,), rk1_r=(NT,),
    qkv_s=(NT,), qkv_r=(NT,),
    ag2_s=(2, 20), ag2_r=(2, NT, 2),
    at_s=(NT,), at_r=(NT,),
    rs2_s=(NT,), rs2_r=(NT,), rk2_s=(NT,), rk2_r=(NT,),
)
INPUTS = (
    "lens", "gain", "adapter", "old", "new", "hid", "wq", "wk", "wv", "wo",
    "dn", "qu", "vu", "od", "ou", "kc", "vc",
)


class Refs:
    pass


def dot(a, b):
    return lax.dot_general(a, b, (((1,), (0,)), ((), ())), preferred_element_type=F32)


def dot_nt(a, b):
    return lax.dot_general(a, b, (((1,), (1,)), ((), ())), preferred_element_type=F32)


def remote(src, dst, ssem, rsem, **where):
    return pltpu.make_async_remote_copy(
        src_ref=src, dst_ref=dst, send_sem=ssem, recv_sem=rsem, device_id=where, device_id_type=MESH
    )


def loop(lo, hi, body):
    lax.fori_loop(lo, hi, lambda k, c: (body(k), c)[1], 0)


def peers(me, n, body):
    loop(1, n, lambda k: body(lax.rem(me + k, n)))


def mesh_gather(x, y, ref_of, ssem, rsem):
    def at(p, da, db):
        ax, ay = (da, db) if p == 0 else (db, da)
        return lax.rem(x + ax + SIDE, SIDE) * SIDE + lax.rem(y + ay + SIDE, SIDE)

    count = [0, 0]
    sent = []

    def copy(p, da, db, half, to, idx):
        block = at(p, da, db)
        ref = ref_of(block, p, half)
        return remote(
            ref, ref, ssem.at[p, idx], rsem.at[p, block, half or 0], tp=at(p, *to)
        )

    def send(p, da, db, half, to):
        c = copy(p, da, db, half, to, count[p])
        count[p] += 1
        c.start()
        sent.append(c)

    def wait(p, da, db, half=None):
        copy(p, da, db, half, (1, 0), 0).wait_recv()

    def start():
        for p in range(2):
            for to in ((1, 0), (-1, 0), (0, 1), (0, -1)):
                send(p, 0, 0, None, to)

    def along_b(p, da):
        send(p, da, 0, None, (0, 1))
        send(p, da, 0, None, (0, -1))

    def s1():
        for p in range(2):
            wait(p, -1, 0)
            send(p, -1, 0, 0, (1, 0))
            along_b(p, -1)
        for p in range(2):
            wait(p, 1, 0)
            send(p, 1, 0, 1, (-1, 0))
            along_b(p, 1)

    def s2():
        for p in range(2):
            wait(p, 0, -1)
            send(p, 0, -1, 0, (0, 1))
            wait(p, 0, 1)
            send(p, 0, 1, 1, (0, -1))

    def s3():
        for p in range(2):
            wait(p, 2, 0, 0)
            wait(p, 2, 0, 1)
            along_b(p, 2)

    def s4():
        for da in (-1, 1):
            for p in range(2):
                wait(p, da, -1)
                send(p, da, -1, 0, (0, 1))
                wait(p, da, 1)
                send(p, da, 1, 1, (0, -1))

    def s5():
        for p in range(2):
            wait(p, 0, 2, 0)
            wait(p, 0, 2, 1)

    def s6():
        for p in range(2):
            wait(p, 2, -1)
            send(p, 2, -1, 0, (0, 1))
            wait(p, 2, 1)
            send(p, 2, 1, 1, (0, -1))

    def s7():
        for da in (-1, 1, 2):
            for p in range(2):
                wait(p, da, 2, 0)
                wait(p, da, 2, 1)

    return start, (s1, s2, s3, s4, s5, s6, s7), sent


def kernel(*args):
    names = list(INPUTS) + ["out", "tabs"] + list(SCRATCH) + list(SEMS)
    r = Refs()
    for name, ref in zip(names, args, strict=True):
        setattr(r, name, ref)
    i = lax.axis_index("inst")
    t = lax.axis_index("tp")
    x, y = t // SIDE, lax.rem(t, SIDE)
    core = lax.rem(i, 2)
    sibling = i + 1 - 2 * core

    loads = {}

    def load(name, src, dst):
        c = pltpu.make_async_copy(src, dst, r.ld.at[len(loads)])
        c.start()
        loads[name] = c

    load("hid", r.hid, r.ag.at[t])
    for m in ("dn", "qu", "vu", "od", "ou"):
        load(m, getattr(r, m), getattr(r, m + "v"))

    bar = pltpu.get_barrier_semaphore()

    def hello(axis, p):
        pl.semaphore_signal(bar, inc=1, device_id={axis: p}, device_id_type=MESH)

    peers(t, NT, lambda p: hello("tp", p))
    peers(i, NI, lambda p: hello("inst", p))

    sub = lax.broadcasted_iota(jnp.int32, (128, 128), 0)
    lan = lax.broadcasted_iota(jnp.int32, (128, 128), 1)
    eye = sub == lan

    def to_column(v):
        return jnp.sum(jnp.where(eye, v, 0.0), axis=1, keepdims=True)

    def to_row(v):
        return jnp.sum(jnp.where(eye, v, 0.0), axis=0, keepdims=True)

    old, new = r.old[...], r.new[...]
    goes = ((old >> 3) == i) & ((new >> 3) == sub) & (sub < NI)
    comes = (new == i * SLOTS + sub - NI) & (sub >= NI) & (sub < NI + SLOTS)
    table = jnp.where(goes, old & 7, 0) + jnp.where(comes, old >> 3, 0)
    table = jnp.sum(table, axis=1, keepdims=True)
    table = jnp.sum(jnp.where(eye, table, 0), axis=0, keepdims=True)
    r.tabv[...] = jnp.broadcast_to(table, (8, 128))
    load("tabs", r.tabv, r.tabs)
    named = to_column(r.adapter[...].astype(F32)) == lan.astype(F32)
    slot_column = jnp.sum(jnp.where(named, new.astype(F32), 0.0), axis=1, keepdims=True)
    slot_column = jnp.broadcast_to(slot_column - (i * SLOTS).astype(F32), (128, 128))
    for p in range(NT):
        for s in range(2):
            r.rmask[p * OWN + s * 8 : p * OWN + s * 8 + 8] = slot_column[8 * p : 8 * p + 8]

    def entry(n, top):
        return jnp.clip(r.tabs[0, n], 0, top - 1)

    loads["hid"].wait()
    parts = []
    for s in range(2):
        h = r.ag[t, s].astype(F32)
        parts.append(to_row(jnp.sum(h * h, axis=1, keepdims=True)))
    gain = r.gain[...].astype(F32)
    r.ssb[t] = jnp.concatenate(parts + [gain, jnp.zeros((2, 128), F32)], axis=0)

    pl.semaphore_wait(bar, NT + NI - 2)

    def ss_copy(src_block, to):
        return remote(
            r.ssb.at[src_block], r.ssb.at[src_block], r.ss_s.at[to], r.ss_r.at[src_block], tp=to
        )

    peers(t, NT, lambda p: ss_copy(t, p).start())

    def ag_ref(block, p, half):
        if half is None:
            return r.ag.at[block, p]
        return r.ag.at[block, p, pl.ds(half * 64, 64)]

    start, steps, sent1 = mesh_gather(x, y, ag_ref, r.ag_s, r.ag_r)
    start()
    loads["tabs"].wait()

    kinds = ("dn", "qu", "vu", "od", "ou")

    def z_copy(m, block, slot, to):
        st, rc = getattr(r, kinds[m] + "s"), getattr(r, kinds[m] + "r")
        return remote(st.at[block], rc.at[slot], r.z_s.at[m, to], r.z_r.at[m, slot], inst=to)

    def send_kind(m):
        loads[kinds[m]].wait()
        have, st, rc = (getattr(r, kinds[m] + e) for e in "vsr")
        if kinds[m] == "vu":
            st[...] = jnp.zeros_like(st)

        def stage(j):
            block = have[entry(j, SLOTS)]
            if kinds[m] == "vu":
                st[j, :, 0:64] = block
            else:
                st[j] = block

        loop(0, NI, stage)
        peers(i, NI, lambda p: z_copy(m, p, i, p).start())
        rc[i] = st[i]

    send_kind(0)

    for m in range(1, 5):
        send_kind(m)

    load("wq", r.wq, r.wqv)
    r.wkv[...] = jnp.zeros_like(r.wkv)
    lane0 = pl.multiple_of(32 * lax.rem(t, 4), 32)
    load("wk", r.wk, r.wkv.at[pl.ds(lane0, 32)])
    load("wv", r.wv, r.wkv.at[pl.ds(128 + lane0, 32)])
    load("kc", r.kc, r.kext.at[:, pl.ds(0, LMAX)])
    load("vc", r.vc, r.vext.at[:, pl.ds(0, LMAX)])
    steps[0]()
    steps[1]()
    for ref in (r.qcat, r.vcat, r.oucat, r.qacc, r.kvacc, r.rs2s):
        ref[...] = jnp.zeros_like(ref)

    def wo_src(p):
        return r.wo.at[pl.ds(core * 128, 128), pl.ds(pl.multiple_of(p * SH, SH), SH)]

    def wo_copy(row, to):
        return remote(wo_src(to), r.wof.at[row, core], r.wo_s.at[to], r.wo_r.at[row], tp=to)

    load("wo", wo_src(t), r.wof.at[t, core])
    for n, step in enumerate(steps[2:]):
        step()
        for dx, dy in WO_ORDER[3 * n : 3 * n + 3]:
            ox, oy = dx + core * (dy - dx), dy + core * (dx - dy)
            p = lax.rem(x + ox, SIDE) * SIDE + lax.rem(y + oy, SIDE)
            wo_copy(t, p).start()

    peers(t, NT, lambda p: ss_copy(p, p).wait_recv())
    total = jnp.sum(r.ssb[...], axis=0)
    scale = [
        lax.rsqrt(to_column(total[s : s + 1, :]) * (1.0 / D) + NORM_EPS) for s in range(2)
    ]
    for b in range(NT):
        r.gains[b] = jnp.concatenate([r.ssb[b, 2 + q : 3 + q, :] for q in range(4)], axis=1)

    def normalise(b, dst):
        gain = r.gains[b]
        n0, n1 = (r.ag[b, s].astype(F32) * scale[s] * gain for s in range(2))
        for p in range(NT):
            rows = slice(8 * p, 8 * p + 8)
            dst[p * OWN : (p + 1) * OWN] = jnp.concatenate([n0[rows], n1[rows]], axis=0).astype(BF16)

    normalise(t, r.mine)
    for name in ("wq", "wk", "wv"):
        loads[name].wait()

    def project(b):
        cols = pl.ds(pl.multiple_of(b * SH, SH), SH)
        normalise(b, r.nrm)
        block = r.nrm[...]
        r.qacc[...] += dot(block, r.wqv[cols, :])
        r.kvacc[...] += dot_nt(block, r.wkv[:, cols])

    loop(0, NT, project)

    loads["wo"].wait()
    peers(t, NT, lambda p: wo_copy(p, p).wait_recv())
    sib = remote(
        r.wof.at[:, core], r.wof.at[:, core], r.sib_s.at[0], r.sib_r.at[0], inst=sibling
    )
    sib.start()

    def z_wait(m):
        peers(i, NI, lambda p: z_copy(m, p, p, p).wait_recv())

    def reduce_rows(own, send, recv, gathered, s1, r1, s2, r2):
        def c1(block, slot, to):
            return remote(send.at[block], recv.at[slot], s1.at[to], r1.at[slot], tp=to)

        def c2(slot, to):
            return remote(gathered.at[slot], gathered.at[slot], s2.at[to], r2.at[slot], tp=to)

        peers(t, NT, lambda p: c1(p, t, p).start())
        recv[t] = send[t]
        peers(t, NT, lambda p: c1(p, p, p).wait_recv())
        gathered[t] = jnp.sum(recv[...], axis=0).astype(BF16)
        peers(t, NT, lambda p: c2(t, p).start())
        peers(t, NT, lambda p: c2(p, p).wait_recv())

        def finish():
            peers(t, NT, lambda p: c1(p, p, p).wait_send())
            peers(t, NT, lambda p: c2(p, p).wait_send())

        return gathered[...].reshape(R2, 128).astype(F32), finish

    slot_of_row = r.rmask[...]
    z_wait(0)
    mine = r.mine[...]
    part = jnp.zeros((R2, 128), F32)
    for k in range(SLOTS):
        got = dot(mine, r.dnr[entry(NI + k, NI)])
        part = jnp.where(slot_of_row == float(k), got, part)
    r.rs1s[...] = part.reshape(NT, OWN, 128)
    rank, finish1 = reduce_rows(
        t, r.rs1s, r.rs1r, r.rk1, r.rs1_s, r.rs1_r, r.rk1_s, r.rk1_r
    )
    rolled = pltpu.roll(rank, 64, 1)
    for k in range(SLOTS):
        cols = slice(k * 128, (k + 1) * 128)
        r.rall[:, cols] = jnp.where(slot_of_row == float(k), rank, 0.0).astype(BF16)
        r.rall2[:, cols] = jnp.where(slot_of_row == float(k), rolled, 0.0).astype(BF16)

    z_wait(1)
    z_wait(2)
    for k in range(SLOTS):
        r.qcat[k * 128 : k * 128 + 64] = r.qur[entry(NI + k, NI)]
        r.vcat[pl.ds(lane0, 32), k * 128 : (k + 1) * 128] = r.vur[entry(NI + k, NI)]
    query = r.qacc[...] + ADAPTER_SCALING * dot(r.rall[...], r.qcat[...])
    fresh_value = r.kvacc[:, 128:] + ADAPTER_SCALING * dot_nt(r.rall2[...], r.vcat[...])
    r.qkvs[:, :, 0:256] = query.astype(BF16).reshape(NT, OWN, 256)
    r.qkvs[:, :, 256:384] = r.kvacc[:, :128].astype(BF16).reshape(NT, OWN, 128)
    r.qkvs[:, :, 384:512] = fresh_value.astype(BF16).reshape(NT, OWN, 128)

    def qkv_copy(block, slot, to):
        return remote(r.qkvs.at[block], r.qkvr.at[slot], r.qkv_s.at[to], r.qkv_r.at[slot], tp=to)

    peers(t, NT, lambda p: qkv_copy(p, t, p).start())
    r.qkvr[t] = r.qkvs[t]

    row = lax.broadcasted_iota(jnp.int32, (OWN, HD), 0)
    lane = lax.broadcasted_iota(jnp.int32, (OWN, HD), 1)
    step_of_row = row // 8
    positions = step_of_row
    for b in range(8):
        positions = positions + jnp.where(lax.rem(row, 8) == b, r.lens[b], 0)
    freq = jnp.exp(lax.rem(lane, 64).astype(F32) * (-math.log(ROPE_BASE) / 64))
    angle = positions.astype(F32) * freq
    cos2 = jnp.cos(angle)
    sin2 = jnp.sin(angle)
    sin2 = jnp.where(lane < 64, -sin2, sin2)

    def rotate(v):
        return v * cos2 + pltpu.roll(v, 64, 1) * sin2

    peers(t, NT, lambda p: qkv_copy(p, p, p).wait_recv())
    loads["kc"].wait()
    loads["vc"].wait()
    for b in range(NT):
        for h in range(2):
            head = r.qkvr[b, :, h * HD : (h + 1) * HD].astype(F32)
            r.q2[pl.ds(2 * b + h, OWN, stride=HEADS)] = rotate(head)
    for g in range(4):
        cols = slice(g * HD, (g + 1) * HD)
        key = jnp.zeros((OWN, HD), F32)
        val = jnp.zeros((OWN, HD), F32)
        for b in range(4 * g, 4 * g + 4):
            key += r.qkvr[b, :, 256:384].astype(F32)
            val += r.qkvr[b, :, 384:512].astype(F32)
        key = rotate(key)
        for b in range(8):
            for v, ref in ((key, r.kext), (val, r.vext)):
                ref[b, LMAX:LPAD, cols] = jnp.where(
                    row == 0, v[b : b + 1], jnp.where(row == 1, v[8 + b : 9 + b], 0.0)
                ).astype(BF16)
    for b in range(8):
        for g in range(4):
            lo = [(s * 8 + b) * HEADS + 8 * g for s in range(2)]
            q = jnp.concatenate([r.q2[o : o + 8] for o in lo], axis=0).astype(BF16)
            score = dot_nt(q, r.kext[b, :, g * HD : (g + 1) * HD])
            r.sc[(b * 4 + g) * OWN : (b * 4 + g + 1) * OWN] = score * (1.0 / math.sqrt(HD))
    at_key = lax.broadcasted_iota(jnp.int32, (64, LPAD), 1)
    at_step = lax.rem(lax.broadcasted_iota(jnp.int32, (64, LPAD), 0) // 8, 2)
    for b in range(8):
        rows = slice(b * 64, (b + 1) * 64)
        live = at_key < jnp.where(at_key < LMAX, r.lens[b], LMAX + 1 + at_step)
        score = jnp.where(live, r.sc[rows], -jnp.inf)
        power = jnp.exp(score - jnp.max(score, axis=1, keepdims=True))
        r.wt[rows] = (power / jnp.sum(power, axis=1, keepdims=True)).astype(BF16)
    for b in range(8):
        for g in range(4):
            weight = r.wt[(b * 4 + g) * OWN : (b * 4 + g + 1) * OWN]
            mix = dot(weight, r.vext[b, :, g * HD : (g + 1) * HD])
            for s in range(2):
                lo = (s * 8 + b) * HEADS + 8 * g
                r.o2[lo : lo + 8] = mix[s * 8 : s * 8 + 8]
    for h in range(HEADS):
        r.ag2[t, :, h * HD : (h + 1) * HD] = r.o2[pl.ds(h, OWN, stride=HEADS)].astype(BF16)

    def at_copy(cols_of, slot, to):
        src = r.ag2.at[t, :, pl.ds(pl.multiple_of(cols_of * 256, 256), 256)]
        return remote(src, r.attd.at[slot], r.at_s.at[to], r.at_r.at[slot], tp=to)

    peers(t, NT, lambda p: at_copy(p, t, p).start())

    def ag2_ref(block, p, half):
        if half is None:
            return r.ag2.at[block, :, pl.ds(p * 2048, 2048)]
        return r.ag2.at[block, :, pl.ds(p * 2048 + half * 1024, 1024)]

    start, steps, sent2 = mesh_gather(x, y, ag2_ref, r.ag2_s, r.ag2_r)
    start()
    r.attd[t] = r.ag2[t, :, pl.ds(pl.multiple_of(t * 256, 256), 256)]
    z_wait(3)
    steps[0]()
    steps[1]()
    peers(t, NT, lambda p: at_copy(p, p, p).wait_recv())
    heads = r.attd[...].reshape(R2, 256)
    part = jnp.zeros((R2, 64), F32)
    for k in range(SLOTS):
        got = dot_nt(heads, r.odr[entry(NI + k, NI)])
        part = jnp.where(slot_of_row[:, :64] == float(k), got, part)
    r.rs2s[:, :, 0:64] = part.reshape(NT, OWN, 64)
    for step in steps[2:4]:
        step()
    rank, finish2 = reduce_rows(
        t, r.rs2s, r.rs2r, r.rk2, r.rs2_s, r.rs2_r, r.rk2_s, r.rk2_r
    )
    for k in range(SLOTS):
        cols = slice(k * 128, (k + 1) * 128)
        r.rall[:, cols] = jnp.where(slot_of_row == float(k), rank, 0.0).astype(BF16)
    for step in steps[4:]:
        step()

    sib_in = remote(
        r.wof.at[:, 1 - core], r.wof.at[:, 1 - core], r.sib_s.at[0], r.sib_r.at[0], inst=sibling
    )
    sib_in.wait_recv()
    r.oacc[...] = jnp.zeros_like(r.oacc)

    def out_chunk(c):
        lhs = r.ag2[:, :, pl.ds(pl.multiple_of(c * 512, 512), 512)].reshape(R2, 512)
        rhs = r.wof[pl.ds(c * 2, 2)].reshape(512, SH)
        r.oacc[...] += dot(lhs, rhs)

    loop(0, 8, out_chunk)
    z_wait(4)
    for k in range(SLOTS):
        r.oucat[k * 128 : k * 128 + 64] = r.our[entry(NI + k, NI)]
    res = r.oacc[...] + ADAPTER_SCALING * dot(r.rall[...], r.oucat[...])
    for p in range(NT):
        for s in range(2):
            lo = p * OWN + s * 8
            r.oacc[s * ROWS + p * 8 : s * ROWS + p * 8 + 8] = res[lo : lo + 8]
    for s in range(2):
        r.out[s] = r.oacc[s * ROWS : (s + 1) * ROWS].astype(BF16)

    peers(t, NT, lambda p: ss_copy(p, p).wait_send())
    for m in range(5):
        peers(i, NI, lambda p, m=m: z_copy(m, p, p, p).wait_send())
    for c in sent1 + sent2:
        c.wait_send()
    peers(t, NT, lambda p: wo_copy(p, p).wait_send())
    sib.wait_send()
    peers(t, NT, lambda p: qkv_copy(p, p, p).wait_send())
    peers(t, NT, lambda p: at_copy(p, p, p).wait_send())
    finish1()
    finish2()


def local(
    hidden_in,
    norm_gain,
    query_weight,
    w_key,
    value_weight,
    w_output,
    paired_down_matrices,
    query_up_matrices,
    value_up_matrices,
    output_down_matrices,
    output_up_matrices,
    key_cache,
    value_cache,
    cache_lengths,
    row_adapter,
    old_slot,
    new_slot,
):
    smem = pl.BlockSpec(memory_space=pltpu.SMEM)
    vmem = pl.BlockSpec(memory_space=pltpu.VMEM)
    hbm = pl.BlockSpec(memory_space=pl.ANY)
    return pl.pallas_call(
        kernel,
        out_shape=jax.ShapeDtypeStruct((2, ROWS, SH), BF16),
        in_specs=[smem] + [vmem] * 4 + [hbm] * 12,
        out_specs=vmem,
        scratch_shapes=[pltpu.SMEM((8, 128), jnp.int32)]
        + [pltpu.VMEM(*s) for s in SCRATCH.values()]
        + [pltpu.SemaphoreType.DMA(s) for s in SEMS.values()],
        compiler_params=pltpu.CompilerParams(
            collective_id=0, has_side_effects=True, vmem_limit_bytes=58 * 2**20
        ),
        name="decode_block",
    )(
        cache_lengths,
        norm_gain.reshape(4, 128),
        row_adapter.reshape(1, ROWS),
        old_slot.reshape(1, -1),
        new_slot.reshape(1, -1),
        hidden_in,
        query_weight,
        w_key.T,
        value_weight.T,
        w_output,
        paired_down_matrices,
        query_up_matrices,
        jnp.swapaxes(value_up_matrices, 1, 2),
        output_down_matrices,
        output_up_matrices,
        key_cache,
        value_cache,
    )


def solution(mesh):
    placed = (
        P(None, "inst", "tp"),
        P("tp"),
        P(None, "tp"),
        P(None, "tp"),
        P(None, "tp"),
        P("tp", None),
        P("inst", "tp", None),
        P("inst", None, "tp"),
        P("inst", None, "tp"),
        P("inst", None, "tp"),
        P("inst", None, "tp"),
        P(("inst", "tp"), None, None),
        P(("inst", "tp"), None, None),
        P(("inst", "tp")),
        P("inst"),
        P(),
        P(),
    )
    return jax.shard_map(
        local, mesh=mesh, in_specs=placed, out_specs=P(None, "inst", "tp"), check_vma=False
    )
```

```python
import functools
import math

import jax
import jax.numpy as jnp
from jax import lax
from jax.experimental import pallas as pl
from jax.experimental.pallas import tpu as pltpu
from jax.sharding import PartitionSpec as P

MESH = pl.DeviceIdType.MESH
F32, BF16 = jnp.float32, jnp.bfloat16

NT = 16
NI = 16
NZ = 8
SIDE = 4
D = 8192
SH = 512
ROWS = 128
R2 = 256
OWN = 16
HEADS = 32
HD = 128
SLOTS = 8
LMAX = 64
LPAD = 80
ADAPTER_SCALING = 0.5
NORM_EPS = 1e-05
ROPE_BASE = 500000.0

WO_ORDER = (
    (1, 0), (0, 3), (3, 0), (0, 1), (1, 1), (3, 3), (1, 3), (3, 1),
    (2, 0), (0, 2), (2, 1), (1, 2), (2, 3), (3, 2), (2, 2),
)

SCRATCH = dict(
    tabv=((8, 128), jnp.int32),
    rmask=((R2, 128), F32),
    ag=((NT, 2, ROWS, SH), BF16),
    nrm=((R2, SH), BF16),
    gains=((NT, 1, SH), F32),
    sc=((8 * 64, LPAD), F32),
    wt=((8 * 64, LPAD), BF16),
    wqv=((D, 256), BF16),
    wkv=((256, D), BF16),
    wof=((NT, 2, 128, SH), BF16),
    dn2=((SLOTS, SH, 256), BF16),
    zb=((NZ, 2, ROWS, SH), BF16),
    zsb=((NZ, 8, 128), F32),
    zmask=((R2, 128), F32),
    ps=((NT, NZ, OWN, 128), BF16),
    pr=((NT, NZ, OWN, 128), BF16),
    rrs=((NZ, OWN, 128), BF16),
    rr=((NZ, OWN, 128), BF16),
    quv=((SLOTS, 64, 256), BF16),
    vuv=((SLOTS, 32, 64), BF16),
    odv=((SLOTS, 64, 256), BF16),
    ouv=((SLOTS, 64, SH), BF16),
    qus=((NI, 64, 256), BF16),
    vus=((NI, 32, 128), BF16),
    ods=((NI, 64, 256), BF16),
    ous=((NI, 64, SH), BF16),
    qur=((NI, 64, 256), BF16),
    vur=((NI, 32, 128), BF16),
    odr=((NI, 64, 256), BF16),
    our=((NI, 64, SH), BF16),
    qcat=((SLOTS * 128, 256), BF16),
    vcat=((128, SLOTS * 128), BF16),
    oucat=((SLOTS * 128, SH), BF16),
    rall=((R2, SLOTS * 128), BF16),
    rall2=((R2, SLOTS * 128), BF16),
    kext=((8, LPAD, 512), BF16),
    vext=((8, LPAD, 512), BF16),
    ssb=((NT, 8, 128), F32),
    rk1=((NT, OWN, 128), BF16),
    rs2s=((NT, OWN, 128), F32),
    rs2r=((NT, OWN, 128), F32),
    rk2=((NT, OWN, 128), BF16),
    qacc=((R2, 256), F32),
    kvacc=((R2, 256), F32),
    qkvs=((NT, OWN, 512), BF16),
    qkvr=((NT, OWN, 512), BF16),
    q2=((OWN * HEADS, HD), F32),
    o2=((OWN * HEADS, HD), F32),
    ag2=((NT, OWN, HEADS * HD), BF16),
    attd=((NT, OWN, 256), BF16),
    oacc=((R2, SH), F32),
)
SEMS = dict(
    ld=(16,),
    ss_s=(NT,), ss_r=(NT,),
    ag_s=(2, 20), ag_r=(2, NT, 2),
    z_s=(4, NI), z_r=(4, NI),
    zg_s=(14,), zg_r=(NZ, 2), zs_s=(NZ,), zs_r=(NZ,), dn_s=(1,), dn_r=(1,),
    pr_s=(NT,), pr_r=(NT,), rr_s=(NZ,), rr_r=(NZ,),
    wo_s=(NT,), wo_r=(NT,), sib_s=(1,), sib_r=(1,),
    rk1_s=(NT,), rk1_r=(NT,),
    qkv_s=(NT,), qkv_r=(NT,),
    ag2_s=(2, 20), ag2_r=(2, NT, 2),
    at_s=(NT,), at_r=(NT,),
    rs2_s=(NT,), rs2_r=(NT,), rk2_s=(NT,), rk2_r=(NT,),
)
INPUTS = (
    "lens", "gain", "adapter", "old", "new", "hid", "wq", "wk", "wv", "wo",
    "dn", "qu", "vu", "od", "ou", "kc", "vc",
)


class Refs:
    pass


def dot(a, b):
    return lax.dot_general(a, b, (((1,), (0,)), ((), ())), preferred_element_type=F32)


def dot_nt(a, b):
    return lax.dot_general(a, b, (((1,), (1,)), ((), ())), preferred_element_type=F32)


def remote(src, dst, ssem, rsem, **where):
    return pltpu.make_async_remote_copy(
        src_ref=src, dst_ref=dst, send_sem=ssem, recv_sem=rsem, device_id=where, device_id_type=MESH
    )


def loop(lo, hi, body):
    lax.fori_loop(lo, hi, lambda k, c: (body(k), c)[1], 0)


def peers(me, n, body):
    loop(1, n, lambda k: body(lax.rem(me + k, n)))


def mesh_gather(x, y, ref_of, ssem, rsem):
    def at(p, da, db):
        ax, ay = (da, db) if p == 0 else (db, da)
        return lax.rem(x + ax + SIDE, SIDE) * SIDE + lax.rem(y + ay + SIDE, SIDE)

    count = [0, 0]
    sent = []

    def copy(p, da, db, half, to, idx):
        block = at(p, da, db)
        ref = ref_of(block, p, half)
        return remote(
            ref, ref, ssem.at[p, idx], rsem.at[p, block, half or 0], tp=at(p, *to)
        )

    def send(p, da, db, half, to):
        c = copy(p, da, db, half, to, count[p])
        count[p] += 1
        c.start()
        sent.append(c)

    def wait(p, da, db, half=None):
        copy(p, da, db, half, (1, 0), 0).wait_recv()

    def start():
        for p in range(2):
            for to in ((1, 0), (-1, 0), (0, 1), (0, -1)):
                send(p, 0, 0, None, to)

    def along_b(p, da):
        send(p, da, 0, None, (0, 1))
        send(p, da, 0, None, (0, -1))

    def s1():
        for p in range(2):
            wait(p, -1, 0)
            send(p, -1, 0, 0, (1, 0))
            along_b(p, -1)
        for p in range(2):
            wait(p, 1, 0)
            send(p, 1, 0, 1, (-1, 0))
            along_b(p, 1)

    def s2():
        for p in range(2):
            wait(p, 0, -1)
            send(p, 0, -1, 0, (0, 1))
            wait(p, 0, 1)
            send(p, 0, 1, 1, (0, -1))

    def s3():
        for p in range(2):
            wait(p, 2, 0, 0)
            wait(p, 2, 0, 1)
            along_b(p, 2)

    def s4():
        for da in (-1, 1):
            for p in range(2):
                wait(p, da, -1)
                send(p, da, -1, 0, (0, 1))
                wait(p, da, 1)
                send(p, da, 1, 1, (0, -1))

    def s5():
        for p in range(2):
            wait(p, 0, 2, 0)
            wait(p, 0, 2, 1)

    def s6():
        for p in range(2):
            wait(p, 2, -1)
            send(p, 2, -1, 0, (0, 1))
            wait(p, 2, 1)
            send(p, 2, 1, 1, (0, -1))

    def s7():
        for da in (-1, 1, 2):
            for p in range(2):
                wait(p, da, 2, 0)
                wait(p, da, 2, 1)

    return start, (s1, s2, s3, s4, s5, s6, s7), sent


def kernel(*args):
    names = list(INPUTS) + ["out", "tabs"] + list(SCRATCH) + list(SEMS)
    r = Refs()
    for name, ref in zip(names, args, strict=True):
        setattr(r, name, ref)
    i = lax.axis_index("inst")
    t = lax.axis_index("tp")
    x, y = t // SIDE, lax.rem(t, SIDE)
    core = lax.rem(i, 2)
    zc = i // 2
    sibling = i + 1 - 2 * core

    loads = {}

    def load(name, src, dst):
        c = pltpu.make_async_copy(src, dst, r.ld.at[len(loads)])
        c.start()
        loads[name] = c

    load("hid", r.hid, r.ag.at[t])
    half0 = pl.multiple_of(core * 128, 128)
    half1 = pl.multiple_of(128 - core * 128, 128)
    load("dn", r.dn, r.dn2.at[:, :, pl.ds(half0, 128)])
    for m in ("qu", "vu", "od", "ou"):
        load(m, getattr(r, m), getattr(r, m + "v"))

    bar = pltpu.get_barrier_semaphore()

    def hello(axis, p):
        pl.semaphore_signal(bar, inc=1, device_id={axis: p}, device_id_type=MESH)

    peers(t, NT, lambda p: hello("tp", p))
    peers(i, NI, lambda p: hello("inst", p))

    loads["hid"].wait()
    pl.semaphore_wait(bar, NT + NI - 2)

    def ag_ref(block, p, half):
        if half is None:
            return r.ag.at[block, p]
        return r.ag.at[block, p, pl.ds(half * 64, 64)]

    start, steps, sent1 = mesh_gather(x, y, ag_ref, r.ag_s, r.ag_r)
    start()

    def chip(d):
        return lax.rem(zc + d + NZ, NZ)

    def zg_copy(d, half, to, idx):
        block = chip(d)
        src, dst = (r.ag.at[t] if d == 0 else r.zb.at[block]), r.zb.at[block]
        if half is not None:
            src, dst = src.at[half], dst.at[half]
        return remote(
            src, dst, r.zg_s.at[idx], r.zg_r.at[block, half or 0], inst=chip(to) * 2 + core
        )

    sent_z = []

    def zg_send(*what):
        c = zg_copy(*what, len(sent_z))
        c.start()
        sent_z.append(c)

    def zg_wait(d, half=None):
        zg_copy(d, half, 1, 0).wait_recv()

    def zg_pass(d, order):
        for n in order:
            for side in (-1, 1):
                half = n if side < 0 else 1 - n
                zg_wait(side * d, half)
                if d < 3 or n == 0:
                    zg_send(side * d, half, -side)

    for n in range(2):
        zg_send(0, n, 1)
        zg_send(0, 1 - n, -1)
    dn_out = remote(
        r.dn, r.dn2.at[:, :, pl.ds(half0, 128)], r.dn_s.at[0], r.dn_r.at[0], inst=sibling
    )
    dn_out.start()
    r.zb[zc] = r.ag[t]
    sub = lax.broadcasted_iota(jnp.int32, (128, 128), 0)
    lan = lax.broadcasted_iota(jnp.int32, (128, 128), 1)
    eye = sub == lan

    def to_column(v):
        return jnp.sum(jnp.where(eye, v, 0.0), axis=1, keepdims=True)

    def to_row(v):
        return jnp.sum(jnp.where(eye, v, 0.0), axis=0, keepdims=True)

    parts = []
    for s in range(2):
        h = r.ag[t, s].astype(F32)
        parts.append(to_row(jnp.sum(h * h, axis=1, keepdims=True)))
    gain = r.gain[...].astype(F32)
    r.ssb[t] = jnp.concatenate(parts + [gain, jnp.zeros((2, 128), F32)], axis=0)

    def ss_copy(src_block, to):
        return remote(
            r.ssb.at[src_block], r.ssb.at[src_block], r.ss_s.at[to], r.ss_r.at[src_block], tp=to
        )

    peers(t, NT, lambda p: ss_copy(t, p).start())


    old, new = r.old[...], r.new[...]
    goes = ((old >> 3) == i) & ((new >> 3) == sub) & (sub < NI)
    comes = (new == i * SLOTS + sub - NI) & (sub >= NI) & (sub < NI + SLOTS)
    table = jnp.where(goes, old & 7, 0) + jnp.where(comes, old >> 3, 0)
    table = jnp.sum(table, axis=1, keepdims=True)
    table = jnp.sum(jnp.where(eye, table, 0), axis=0, keepdims=True)
    r.tabv[...] = jnp.broadcast_to(table, (8, 128))
    load("tabs", r.tabv, r.tabs)
    named = to_column(r.adapter[...].astype(F32)) == lan.astype(F32)
    slot_column = jnp.sum(jnp.where(named, new.astype(F32), 0.0), axis=1, keepdims=True)
    old_row = to_row(
        jnp.sum(jnp.where(named, old.astype(F32), 0.0), axis=1, keepdims=True)
    )
    slot_column = jnp.broadcast_to(slot_column - (i * SLOTS).astype(F32), (128, 128))
    for p in range(NT):
        for s in range(2):
            r.rmask[p * OWN + s * 8 : p * OWN + s * 8 + 8] = slot_column[8 * p : 8 * p + 8]

    def entry(n, top):
        return jnp.clip(r.tabs[0, n], 0, top - 1)

    steps[0]()
    zg_pass(1, (0,))
    loads["tabs"].wait()

    kinds = ("qu", "vu", "od", "ou")

    def z_copy(m, block, slot, to):
        st, rc = getattr(r, kinds[m] + "s"), getattr(r, kinds[m] + "r")
        return remote(st.at[block], rc.at[slot], r.z_s.at[m, to], r.z_r.at[m, slot], inst=to)

    def stage_kind(m):
        loads[kinds[m]].wait()
        have, st, rc = (getattr(r, kinds[m] + e) for e in "vsr")
        if kinds[m] == "vu":
            st[...] = jnp.zeros_like(st)

        def stage(j):
            block = have[entry(j, SLOTS)]
            if kinds[m] == "vu":
                st[j, :, 0:64] = block
            else:
                st[j] = block

        loop(0, NI, stage)
        rc[i] = st[i]

    def send_kind(m):
        peers(i, NI, lambda p: z_copy(m, p, i, p).start())

    def z_wait(m):
        peers(i, NI, lambda p: z_copy(m, p, p, p).wait_recv())

    for m in range(4):
        stage_kind(m)

    peers(t, NT, lambda p: ss_copy(p, p).wait_recv())
    total = jnp.sum(r.ssb[...], axis=0)
    r.zsb[zc] = jnp.concatenate([total[0:2], old_row, jnp.zeros((5, 128), F32)], axis=0)

    def zs_copy(block, to):
        return remote(
            r.zsb.at[block], r.zsb.at[block], r.zs_s.at[to], r.zs_r.at[block], inst=to * 2 + core
        )

    peers(zc, NZ, lambda p: zs_copy(zc, p).start())
    steps[1]()

    def scales(sums):
        return [
            lax.rsqrt(to_column(sums[s : s + 1, :]) * (1.0 / D) + NORM_EPS) for s in range(2)
        ]

    def normalise(src, scale, gain):
        n0, n1 = (src[s].astype(F32) * scale[s] * gain for s in range(2))
        for p in range(NT):
            rows = slice(8 * p, 8 * p + 8)
            r.nrm[p * OWN : (p + 1) * OWN] = jnp.concatenate(
                [n0[rows], n1[rows]], axis=0
            ).astype(BF16)

    for b in range(NT):
        r.gains[b] = jnp.concatenate([r.ssb[b, 2 + q : 3 + q, :] for q in range(4)], axis=1)
    own_gain = r.gains[t]

    def partial(block):
        sums = r.zsb[block]
        normalise(r.zb.at[block], scales(sums), own_gain)
        slots = to_column(sums[2:3, :]) - (zc * 2 * SLOTS).astype(F32)
        slots = jnp.broadcast_to(slots, (128, 128))
        for p in range(NT):
            for s in range(2):
                lo = p * OWN + s * 8
                r.zmask[lo : lo + 8] = slots[8 * p : 8 * p + 8]
        mask = r.zmask[...]
        rows = r.nrm[...]
        part = jnp.zeros((R2, 128), F32)
        for k in range(SLOTS):
            got = dot(rows, r.dn2[k])
            part = jnp.where(mask == float(k), got[:, :128], part)
            part = jnp.where(mask == float(SLOTS + k), got[:, 128:], part)
        r.ps[:, block] = part.astype(BF16).reshape(NT, OWN, 128)

    load("wq", r.wq, r.wqv)
    r.wkv[...] = jnp.zeros_like(r.wkv)
    lane0 = pl.multiple_of(32 * lax.rem(t, 4), 32)
    load("wk", r.wk, r.wkv.at[pl.ds(lane0, 32)])
    load("wv", r.wv, r.wkv.at[pl.ds(128 + lane0, 32)])
    load("kc", r.kc, r.kext.at[:, pl.ds(0, LMAX)])
    load("vc", r.vc, r.vext.at[:, pl.ds(0, LMAX)])

    zg_pass(1, (1,))
    loads["dn"].wait()
    remote(
        r.dn, r.dn2.at[:, :, pl.ds(half1, 128)], r.dn_s.at[0], r.dn_r.at[0], inst=sibling
    ).wait_recv()
    steps[2]()
    partial(zc)
    zg_pass(2, (0,))
    steps[3]()
    peers(zc, NZ, lambda p: zs_copy(p, p).wait_recv())
    partial(chip(1))
    zg_pass(2, (1,))
    partial(chip(-1))
    zg_pass(3, (0,))
    steps[4]()
    for m in range(2):
        send_kind(m)
    loop(0, 2, lambda k: partial(chip(4 * k - 2)))
    steps[5]()
    zg_pass(3, (1,))
    loop(0, 2, lambda k: partial(chip(6 * k - 3)))
    zg_wait(4, 0)
    zg_wait(4, 1)
    partial(chip(4))

    def in_order(body, part=slice(None)):
        for dx, dy in WO_ORDER[part]:
            ox, oy = dx + core * (dy - dx), dy + core * (dx - dy)
            body(lax.rem(x + ox, SIDE) * SIDE + lax.rem(y + oy, SIDE))

    def wo_src(p):
        return r.wo.at[pl.ds(core * 128, 128), pl.ds(pl.multiple_of(p * SH, SH), SH)]

    def wo_copy(row, to):
        return remote(wo_src(to), r.wof.at[row, core], r.wo_s.at[to], r.wo_r.at[row], tp=to)

    load("wo", wo_src(t), r.wof.at[t, core])

    def send_wo(n):
        in_order(lambda p: wo_copy(t, p).start(), slice(3 * n, 3 * n + 3))

    def pr_copy(block, slot, to):
        return remote(r.ps.at[block], r.pr.at[slot], r.pr_s.at[to], r.pr_r.at[slot], tp=to)

    in_order(lambda p: pr_copy(p, t, p).start())
    r.pr[t] = r.ps[t]
    send_wo(0)
    for ref in (r.qcat, r.vcat, r.oucat, r.qacc, r.kvacc, r.rs2s):
        ref[...] = jnp.zeros_like(ref)
    steps[6]()

    own_scales = scales(total)
    for name in ("wq", "wk", "wv"):
        loads[name].wait()

    def project(b):
        cols = pl.ds(pl.multiple_of(b * SH, SH), SH)
        normalise(r.ag.at[b], own_scales, r.gains[b])
        block = r.nrm[...]
        r.qacc[...] += dot(block, r.wqv[cols, :])
        r.kvacc[...] += dot_nt(block, r.wkv[:, cols])

    loop(0, 6, project)
    peers(t, NT, lambda p: pr_copy(p, p, p).wait_recv())
    sums = jnp.zeros((NZ, OWN, 128), F32)
    for b in range(NT):
        sums += r.pr[b].astype(F32)
    r.rrs[...] = sums.astype(BF16)

    def rr_copy(block, slot, to):
        return remote(
            r.rrs.at[block], r.rr.at[slot], r.rr_s.at[to], r.rr_r.at[slot], inst=to * 2 + core
        )

    peers(zc, NZ, lambda p: rr_copy(p, zc, p).start())
    r.rr[zc] = r.rrs[zc]
    send_wo(1)
    send_kind(2)
    loop(6, 11, project)
    peers(zc, NZ, lambda p: rr_copy(p, p, p).wait_recv())
    r.rk1[t] = jnp.sum(r.rr[...].astype(F32), axis=0).astype(BF16)

    def rk_copy(slot, to):
        return remote(r.rk1.at[slot], r.rk1.at[slot], r.rk1_s.at[to], r.rk1_r.at[slot], tp=to)

    peers(t, NT, lambda p: rk_copy(t, p).start())
    send_wo(2)
    send_kind(3)
    loop(11, NT, project)
    z_wait(0)
    z_wait(1)
    for k in range(SLOTS):
        r.qcat[k * 128 : k * 128 + 64] = r.qur[entry(NI + k, NI)]
        r.vcat[pl.ds(lane0, 32), k * 128 : (k + 1) * 128] = r.vur[entry(NI + k, NI)]
    peers(t, NT, lambda p: rk_copy(p, p).wait_recv())
    rank = r.rk1[...].reshape(R2, 128).astype(F32)
    slot_of_row = r.rmask[...]
    rolled = pltpu.roll(rank, 64, 1)
    for k in range(SLOTS):
        cols = slice(k * 128, (k + 1) * 128)
        r.rall[:, cols] = jnp.where(slot_of_row == float(k), rank, 0.0).astype(BF16)
        r.rall2[:, cols] = jnp.where(slot_of_row == float(k), rolled, 0.0).astype(BF16)

    query = r.qacc[...] + ADAPTER_SCALING * dot(r.rall[...], r.qcat[...])
    fresh_value = r.kvacc[:, 128:] + ADAPTER_SCALING * dot_nt(r.rall2[...], r.vcat[...])
    r.qkvs[:, :, 0:256] = query.astype(BF16).reshape(NT, OWN, 256)
    r.qkvs[:, :, 256:384] = r.kvacc[:, :128].astype(BF16).reshape(NT, OWN, 128)
    r.qkvs[:, :, 384:512] = fresh_value.astype(BF16).reshape(NT, OWN, 128)

    def qkv_copy(block, slot, to):
        return remote(r.qkvs.at[block], r.qkvr.at[slot], r.qkv_s.at[to], r.qkv_r.at[slot], tp=to)

    peers(t, NT, lambda p: qkv_copy(p, t, p).start())
    r.qkvr[t] = r.qkvs[t]
    send_wo(3)
    send_wo(4)

    row = lax.broadcasted_iota(jnp.int32, (OWN, HD), 0)
    lane = lax.broadcasted_iota(jnp.int32, (OWN, HD), 1)
    step_of_row = row // 8
    positions = step_of_row
    for b in range(8):
        positions = positions + jnp.where(lax.rem(row, 8) == b, r.lens[b], 0)
    freq = jnp.exp(lax.rem(lane, 64).astype(F32) * (-math.log(ROPE_BASE) / 64))
    angle = positions.astype(F32) * freq
    cos2 = jnp.cos(angle)
    sin2 = jnp.sin(angle)
    sin2 = jnp.where(lane < 64, -sin2, sin2)

    def rotate(v):
        return v * cos2 + pltpu.roll(v, 64, 1) * sin2

    peers(t, NT, lambda p: qkv_copy(p, p, p).wait_recv())
    loads["kc"].wait()
    loads["vc"].wait()
    for b in range(NT):
        for h in range(2):
            head = r.qkvr[b, :, h * HD : (h + 1) * HD].astype(F32)
            r.q2[pl.ds(2 * b + h, OWN, stride=HEADS)] = rotate(head)
    for g in range(4):
        cols = slice(g * HD, (g + 1) * HD)
        key = jnp.zeros((OWN, HD), F32)
        val = jnp.zeros((OWN, HD), F32)
        for b in range(4 * g, 4 * g + 4):
            key += r.qkvr[b, :, 256:384].astype(F32)
            val += r.qkvr[b, :, 384:512].astype(F32)
        key = rotate(key)
        for b in range(8):
            for v, ref in ((key, r.kext), (val, r.vext)):
                ref[b, LMAX:LPAD, cols] = jnp.where(
                    row == 0, v[b : b + 1], jnp.where(row == 1, v[8 + b : 9 + b], 0.0)
                ).astype(BF16)
    for b in range(8):
        for g in range(4):
            lo = [(s * 8 + b) * HEADS + 8 * g for s in range(2)]
            q = jnp.concatenate([r.q2[o : o + 8] for o in lo], axis=0).astype(BF16)
            score = dot_nt(q, r.kext[b, :, g * HD : (g + 1) * HD])
            r.sc[(b * 4 + g) * OWN : (b * 4 + g + 1) * OWN] = score * (1.0 / math.sqrt(HD))
    at_key = lax.broadcasted_iota(jnp.int32, (64, LPAD), 1)
    at_step = lax.rem(lax.broadcasted_iota(jnp.int32, (64, LPAD), 0) // 8, 2)
    for b in range(8):
        rows = slice(b * 64, (b + 1) * 64)
        live = at_key < jnp.where(at_key < LMAX, r.lens[b], LMAX + 1 + at_step)
        score = jnp.where(live, r.sc[rows], -jnp.inf)
        power = jnp.exp(score - jnp.max(score, axis=1, keepdims=True))
        r.wt[rows] = (power / jnp.sum(power, axis=1, keepdims=True)).astype(BF16)
    for b in range(8):
        for g in range(4):
            weight = r.wt[(b * 4 + g) * OWN : (b * 4 + g + 1) * OWN]
            mix = dot(weight, r.vext[b, :, g * HD : (g + 1) * HD])
            for s in range(2):
                lo = (s * 8 + b) * HEADS + 8 * g
                r.o2[lo : lo + 8] = mix[s * 8 : s * 8 + 8]
    for h in range(HEADS):
        r.ag2[t, :, h * HD : (h + 1) * HD] = r.o2[pl.ds(h, OWN, stride=HEADS)].astype(BF16)

    def at_copy(cols_of, slot, to):
        src = r.ag2.at[t, :, pl.ds(pl.multiple_of(cols_of * 256, 256), 256)]
        return remote(src, r.attd.at[slot], r.at_s.at[to], r.at_r.at[slot], tp=to)

    peers(t, NT, lambda p: at_copy(p, t, p).start())

    def ag2_ref(block, p, half):
        if half is None:
            return r.ag2.at[block, :, pl.ds(p * 2048, 2048)]
        return r.ag2.at[block, :, pl.ds(p * 2048 + half * 1024, 1024)]

    start, steps, sent2 = mesh_gather(x, y, ag2_ref, r.ag2_s, r.ag2_r)
    start()
    r.attd[t] = r.ag2[t, :, pl.ds(pl.multiple_of(t * 256, 256), 256)]
    steps[0]()
    z_wait(2)
    peers(t, NT, lambda p: at_copy(p, p, p).wait_recv())
    heads = r.attd[...].reshape(R2, 256)
    part = jnp.zeros((R2, 64), F32)
    for k in range(SLOTS):
        got = dot_nt(heads, r.odr[entry(NI + k, NI)])
        part = jnp.where(slot_of_row[:, :64] == float(k), got, part)
    r.rs2s[:, :, 0:64] = part.reshape(NT, OWN, 64)

    def c1(block, slot, to):
        return remote(r.rs2s.at[block], r.rs2r.at[slot], r.rs2_s.at[to], r.rs2_r.at[slot], tp=to)

    def c2(slot, to):
        return remote(r.rk2.at[slot], r.rk2.at[slot], r.rk2_s.at[to], r.rk2_r.at[slot], tp=to)

    peers(t, NT, lambda p: c1(p, t, p).start())
    r.rs2r[t] = r.rs2s[t]
    steps[1]()
    steps[2]()
    loads["wo"].wait()
    peers(t, NT, lambda p: wo_copy(p, p).wait_recv())
    sib = remote(
        r.wof.at[:, core], r.wof.at[:, core], r.sib_s.at[0], r.sib_r.at[0], inst=sibling
    )
    sib.start()
    peers(t, NT, lambda p: c1(p, p, p).wait_recv())
    r.rk2[t] = jnp.sum(r.rs2r[...], axis=0).astype(BF16)
    peers(t, NT, lambda p: c2(t, p).start())
    for step in steps[3:]:
        step()

    sib_in = remote(
        r.wof.at[:, 1 - core], r.wof.at[:, 1 - core], r.sib_s.at[0], r.sib_r.at[0], inst=sibling
    )
    sib_in.wait_recv()
    r.oacc[...] = jnp.zeros_like(r.oacc)

    def out_chunk(c):
        lhs = r.ag2[:, :, pl.ds(pl.multiple_of(c * 512, 512), 512)].reshape(R2, 512)
        rhs = r.wof[pl.ds(c * 2, 2)].reshape(512, SH)
        r.oacc[...] += dot(lhs, rhs)

    loop(0, 8, out_chunk)
    peers(t, NT, lambda p: c2(p, p).wait_recv())
    rank = r.rk2[...].reshape(R2, 128).astype(F32)
    for k in range(SLOTS):
        cols = slice(k * 128, (k + 1) * 128)
        r.rall[:, cols] = jnp.where(slot_of_row == float(k), rank, 0.0).astype(BF16)
    z_wait(3)
    for k in range(SLOTS):
        r.oucat[k * 128 : k * 128 + 64] = r.our[entry(NI + k, NI)]
    res = r.oacc[...] + ADAPTER_SCALING * dot(r.rall[...], r.oucat[...])
    for p in range(NT):
        for s in range(2):
            lo = p * OWN + s * 8
            r.oacc[s * ROWS + p * 8 : s * ROWS + p * 8 + 8] = res[lo : lo + 8]
    for s in range(2):
        r.out[s] = r.oacc[s * ROWS : (s + 1) * ROWS].astype(BF16)

    peers(t, NT, lambda p: ss_copy(p, p).wait_send())
    for m in range(4):
        peers(i, NI, lambda p, m=m: z_copy(m, p, p, p).wait_send())
    for c in sent1 + sent2 + sent_z + [dn_out]:
        c.wait_send()
    peers(zc, NZ, lambda p: zs_copy(p, p).wait_send())
    peers(t, NT, lambda p: pr_copy(p, p, p).wait_send())
    peers(zc, NZ, lambda p: rr_copy(p, p, p).wait_send())
    peers(t, NT, lambda p: rk_copy(p, p).wait_send())
    peers(t, NT, lambda p: wo_copy(p, p).wait_send())
    sib.wait_send()
    peers(t, NT, lambda p: qkv_copy(p, p, p).wait_send())
    peers(t, NT, lambda p: at_copy(p, p, p).wait_send())
    peers(t, NT, lambda p: c1(p, p, p).wait_send())
    peers(t, NT, lambda p: c2(p, p).wait_send())


def local(
    hidden_in,
    norm_gain,
    query_weight,
    w_key,
    value_weight,
    w_output,
    paired_down_matrices,
    query_up_matrices,
    value_up_matrices,
    output_down_matrices,
    output_up_matrices,
    key_cache,
    value_cache,
    cache_lengths,
    row_adapter,
    old_slot,
    new_slot,
):
    smem = pl.BlockSpec(memory_space=pltpu.SMEM)
    vmem = pl.BlockSpec(memory_space=pltpu.VMEM)
    hbm = pl.BlockSpec(memory_space=pl.ANY)
    return pl.pallas_call(
        kernel,
        out_shape=jax.ShapeDtypeStruct((2, ROWS, SH), BF16),
        in_specs=[smem] + [vmem] * 4 + [hbm] * 12,
        out_specs=vmem,
        scratch_shapes=[pltpu.SMEM((8, 128), jnp.int32)]
        + [pltpu.VMEM(*s) for s in SCRATCH.values()]
        + [pltpu.SemaphoreType.DMA(s) for s in SEMS.values()],
        compiler_params=pltpu.CompilerParams(
            collective_id=0, has_side_effects=True, vmem_limit_bytes=58 * 2**20
        ),
        name="decode_block",
    )(
        cache_lengths,
        norm_gain.reshape(4, 128),
        row_adapter.reshape(1, ROWS),
        old_slot.reshape(1, -1),
        new_slot.reshape(1, -1),
        hidden_in,
        query_weight,
        w_key.T,
        value_weight.T,
        w_output,
        paired_down_matrices,
        query_up_matrices,
        jnp.swapaxes(value_up_matrices, 1, 2),
        output_down_matrices,
        output_up_matrices,
        key_cache,
        value_cache,
    )


def solution(mesh):
    placed = (
        P(None, "inst", "tp"),
        P("tp"),
        P(None, "tp"),
        P(None, "tp"),
        P(None, "tp"),
        P("tp", None),
        P("inst", "tp", None),
        P("inst", None, "tp"),
        P("inst", None, "tp"),
        P("inst", None, "tp"),
        P("inst", None, "tp"),
        P(("inst", "tp"), None, None),
        P(("inst", "tp"), None, None),
        P(("inst", "tp")),
        P("inst"),
        P(),
        P(),
    )
    return jax.shard_map(
        local, mesh=mesh, in_specs=placed, out_specs=P(None, "inst", "tp"), check_vma=False
    )
```

```python
import functools
import math

import jax
import jax.numpy as jnp
from jax import lax
from jax.experimental import pallas as pl
from jax.experimental.pallas import tpu as pltpu
from jax.sharding import PartitionSpec as P

MESH = pl.DeviceIdType.MESH
F32, BF16 = jnp.float32, jnp.bfloat16

NT = 16
NI = 16
NZ = 8
SIDE = 4
D = 8192
SH = 512
ROWS = 128
R2 = 256
OWN = 16
HEADS = 32
HD = 128
SLOTS = 8
LMAX = 64
LPAD = 80
ADAPTER_SCALING = 0.5
NORM_EPS = 1e-05
ROPE_BASE = 500000.0

WO_ORDER = (
    (1, 0), (0, 3), (3, 0), (0, 1), (1, 1), (3, 3), (1, 3), (3, 1),
    (2, 0), (0, 2), (2, 1), (1, 2), (2, 3), (3, 2), (2, 2),
)

SCRATCH = dict(
    tabv=((8, 128), jnp.int32),
    rmask=((R2, 128), F32),
    ag=((NT, 2, ROWS, SH), BF16),
    nrm=((R2, SH), BF16),
    gains=((NT, 1, SH), F32),
    sc=((8 * 64, LPAD), F32),
    wt=((8 * 64, LPAD), BF16),
    wqv=((D, 256), BF16),
    wkv=((256, D), BF16),
    wof=((NT, 2, 128, SH), BF16),
    dn2=((SLOTS, SH, 256), BF16),
    zb=((NZ, 2, ROWS, SH), BF16),
    zsb=((NZ, 8, 128), F32),
    zmask=((R2, 128), F32),
    ps=((NT, NZ, OWN, 128), BF16),
    pr=((NT, NZ, OWN, 128), BF16),
    rrs=((NZ, OWN, 128), BF16),
    rr=((NZ, OWN, 128), BF16),
    quv=((SLOTS, 64, 256), BF16),
    vuv=((SLOTS, 32, 64), BF16),
    odv=((SLOTS, 64, 256), BF16),
    ouv=((SLOTS, 64, SH), BF16),
    qus=((NI, 64, 256), BF16),
    vus=((NI, 32, 128), BF16),
    ods=((NI, 64, 256), BF16),
    ous=((NI, 64, SH), BF16),
    qur=((NI, 64, 256), BF16),
    vur=((NI, 32, 128), BF16),
    odr=((NI, 64, 256), BF16),
    our=((NI, 64, SH), BF16),
    qcat=((SLOTS * 128, 256), BF16),
    vcat=((128, SLOTS * 128), BF16),
    oucat=((SLOTS * 128, SH), BF16),
    rall=((R2, SLOTS * 128), BF16),
    rall2=((R2, SLOTS * 128), BF16),
    kext=((8, LPAD, 512), BF16),
    vext=((8, LPAD, 512), BF16),
    ssb=((NT, 8, 128), F32),
    rk1=((NT, OWN, 128), BF16),
    rs2s=((NT, OWN, 128), F32),
    rs2r=((NT, OWN, 128), F32),
    rk2=((NT, OWN, 128), BF16),
    qacc=((R2, 256), F32),
    kvacc=((R2, 256), F32),
    qkvs=((NT, OWN, 512), BF16),
    qkvr=((NT, OWN, 512), BF16),
    q2=((OWN * HEADS, HD), F32),
    o2=((OWN * HEADS, HD), F32),
    ag2=((NT, OWN, HEADS * HD), BF16),
    attd=((NT, OWN, 256), BF16),
    oacc=((R2, SH), F32),
)
SEMS = dict(
    ld=(16,),
    ss_s=(NT,), ss_r=(NT,),
    ag_s=(2, 20), ag_r=(2, NT, 2),
    z_s=(4, NI), z_r=(4, NI),
    zg_s=(14,), zg_r=(NZ, 2), zs_s=(NZ,), zs_r=(NZ,), dn_s=(1,), dn_r=(1,),
    pr_s=(NT,), pr_r=(NT,), rr_s=(NZ,), rr_r=(NZ,),
    wo_s=(NT,), wo_r=(NT,), sib_s=(1,), sib_r=(1,),
    rk1_s=(NT,), rk1_r=(NT,),
    qkv_s=(NT,), qkv_r=(NT,),
    ag2_s=(2, 20), ag2_r=(2, NT, 2),
    at_s=(NT,), at_r=(NT,),
    rs2_s=(NT,), rs2_r=(NT,), rk2_s=(NT,), rk2_r=(NT,),
)
INPUTS = (
    "lens", "gain", "adapter", "old", "new", "hid", "wq", "wk", "wv", "wo",
    "dn", "qu", "vu", "od", "ou", "kc", "vc",
)


class Refs:
    pass


def dot(a, b):
    return lax.dot_general(a, b, (((1,), (0,)), ((), ())), preferred_element_type=F32)


def dot_nt(a, b):
    return lax.dot_general(a, b, (((1,), (1,)), ((), ())), preferred_element_type=F32)


def remote(src, dst, ssem, rsem, **where):
    return pltpu.make_async_remote_copy(
        src_ref=src, dst_ref=dst, send_sem=ssem, recv_sem=rsem, device_id=where, device_id_type=MESH
    )


def loop(lo, hi, body):
    lax.fori_loop(lo, hi, lambda k, c: (body(k), c)[1], 0)


def peers(me, n, body):
    loop(1, n, lambda k: body(lax.rem(me + k, n)))


def mesh_gather(x, y, ref_of, ssem, rsem):
    def at(p, da, db):
        ax, ay = (da, db) if p == 0 else (db, da)
        return lax.rem(x + ax + SIDE, SIDE) * SIDE + lax.rem(y + ay + SIDE, SIDE)

    count = [0, 0]
    sent = []

    def copy(p, da, db, half, to, idx):
        block = at(p, da, db)
        ref = ref_of(block, p, half)
        return remote(
            ref, ref, ssem.at[p, idx], rsem.at[p, block, half or 0], tp=at(p, *to)
        )

    def send(p, da, db, half, to):
        c = copy(p, da, db, half, to, count[p])
        count[p] += 1
        c.start()
        sent.append(c)

    def wait(p, da, db, half=None):
        copy(p, da, db, half, (1, 0), 0).wait_recv()

    def start():
        for p in range(2):
            for to in ((1, 0), (-1, 0), (0, 1), (0, -1)):
                send(p, 0, 0, None, to)

    def along_b(p, da):
        send(p, da, 0, None, (0, 1))
        send(p, da, 0, None, (0, -1))

    def s1():
        for p in range(2):
            wait(p, -1, 0)
            send(p, -1, 0, 0, (1, 0))
            along_b(p, -1)
        for p in range(2):
            wait(p, 1, 0)
            send(p, 1, 0, 1, (-1, 0))
            along_b(p, 1)

    def s2():
        for p in range(2):
            wait(p, 0, -1)
            send(p, 0, -1, 0, (0, 1))
            wait(p, 0, 1)
            send(p, 0, 1, 1, (0, -1))

    def s3():
        for p in range(2):
            wait(p, 2, 0, 0)
            wait(p, 2, 0, 1)
            along_b(p, 2)

    def s4():
        for da in (-1, 1):
            for p in range(2):
                wait(p, da, -1)
                send(p, da, -1, 0, (0, 1))
                wait(p, da, 1)
                send(p, da, 1, 1, (0, -1))

    def s5():
        for p in range(2):
            wait(p, 0, 2, 0)
            wait(p, 0, 2, 1)

    def s6():
        for p in range(2):
            wait(p, 2, -1)
            send(p, 2, -1, 0, (0, 1))
            wait(p, 2, 1)
            send(p, 2, 1, 1, (0, -1))

    def s7():
        for da in (-1, 1, 2):
            for p in range(2):
                wait(p, da, 2, 0)
                wait(p, da, 2, 1)

    return start, (s1, s2, s3, s4, s5, s6, s7), sent


def kernel(*args):
    names = list(INPUTS) + ["out", "tabs"] + list(SCRATCH) + list(SEMS)
    r = Refs()
    for name, ref in zip(names, args, strict=True):
        setattr(r, name, ref)
    i = lax.axis_index("inst")
    t = lax.axis_index("tp")
    x, y = t // SIDE, lax.rem(t, SIDE)
    core = lax.rem(i, 2)
    zc = i // 2
    sibling = i + 1 - 2 * core

    loads = {}

    def load(name, src, dst):
        c = pltpu.make_async_copy(src, dst, r.ld.at[len(loads)])
        c.start()
        loads[name] = c

    load("hid", r.hid, r.ag.at[t])
    half0 = pl.multiple_of(core * 128, 128)
    half1 = pl.multiple_of(128 - core * 128, 128)
    load("dn", r.dn, r.dn2.at[:, :, pl.ds(half0, 128)])
    for m in ("qu", "vu", "od", "ou"):
        load(m, getattr(r, m), getattr(r, m + "v"))

    bar = pltpu.get_barrier_semaphore()

    def hello(axis, p):
        pl.semaphore_signal(bar, inc=1, device_id={axis: p}, device_id_type=MESH)

    peers(t, NT, lambda p: hello("tp", p))
    peers(i, NI, lambda p: hello("inst", p))

    loads["hid"].wait()
    pl.semaphore_wait(bar, NT + NI - 2)

    def ag_ref(block, p, half):
        if half is None:
            return r.ag.at[block, p]
        return r.ag.at[block, p, pl.ds(half * 64, 64)]

    start, steps, sent1 = mesh_gather(x, y, ag_ref, r.ag_s, r.ag_r)
    start()

    def chip(d):
        return lax.rem(zc + d + NZ, NZ)

    def zg_copy(d, half, to, idx):
        block = chip(d)
        src, dst = (r.ag.at[t] if d == 0 else r.zb.at[block]), r.zb.at[block]
        if half is not None:
            src, dst = src.at[half], dst.at[half]
        return remote(
            src, dst, r.zg_s.at[idx], r.zg_r.at[block, half or 0], inst=chip(to) * 2 + core
        )

    sent_z = []

    def zg_send(*what):
        c = zg_copy(*what, len(sent_z))
        c.start()
        sent_z.append(c)

    def zg_wait(d, half=None):
        zg_copy(d, half, 1, 0).wait_recv()

    def zg_pass(d, order):
        for n in order:
            for side in (-1, 1):
                half = n if side < 0 else 1 - n
                zg_wait(side * d, half)
                if d < 3 or n == 0:
                    zg_send(side * d, half, -side)

    for n in range(2):
        zg_send(0, n, 1)
        zg_send(0, 1 - n, -1)
    dn_out = remote(
        r.dn, r.dn2.at[:, :, pl.ds(half0, 128)], r.dn_s.at[0], r.dn_r.at[0], inst=sibling
    )
    dn_out.start()
    r.zb[zc] = r.ag[t]
    sub = lax.broadcasted_iota(jnp.int32, (128, 128), 0)
    lan = lax.broadcasted_iota(jnp.int32, (128, 128), 1)
    eye = sub == lan

    def to_column(v):
        return jnp.sum(jnp.where(eye, v, 0.0), axis=1, keepdims=True)

    def to_row(v):
        return jnp.sum(jnp.where(eye, v, 0.0), axis=0, keepdims=True)

    parts = []
    for s in range(2):
        h = r.ag[t, s].astype(F32)
        parts.append(to_row(jnp.sum(h * h, axis=1, keepdims=True)))
    gain = r.gain[...].astype(F32)
    r.ssb[t] = jnp.concatenate(parts + [gain, jnp.zeros((2, 128), F32)], axis=0)

    def ss_copy(src_block, to):
        return remote(
            r.ssb.at[src_block], r.ssb.at[src_block], r.ss_s.at[to], r.ss_r.at[src_block], tp=to
        )

    peers(t, NT, lambda p: ss_copy(t, p).start())


    old, new = r.old[...], r.new[...]
    goes = ((old >> 3) == i) & ((new >> 3) == sub) & (sub < NI)
    comes = (new == i * SLOTS + sub - NI) & (sub >= NI) & (sub < NI + SLOTS)
    table = jnp.where(goes, old & 7, 0) + jnp.where(comes, old >> 3, 0)
    table = jnp.sum(table, axis=1, keepdims=True)
    table = jnp.sum(jnp.where(eye, table, 0), axis=0, keepdims=True)
    r.tabv[...] = jnp.broadcast_to(table, (8, 128))
    load("tabs", r.tabv, r.tabs)
    named = to_column(r.adapter[...].astype(F32)) == lan.astype(F32)
    slot_column = jnp.sum(jnp.where(named, new.astype(F32), 0.0), axis=1, keepdims=True)
    old_row = to_row(
        jnp.sum(jnp.where(named, old.astype(F32), 0.0), axis=1, keepdims=True)
    )
    slot_column = jnp.broadcast_to(slot_column - (i * SLOTS).astype(F32), (128, 128))
    for p in range(NT):
        for s in range(2):
            r.rmask[p * OWN + s * 8 : p * OWN + s * 8 + 8] = slot_column[8 * p : 8 * p + 8]

    def entry(n, top):
        return jnp.clip(r.tabs[0, n], 0, top - 1)

    steps[0]()
    zg_pass(1, (0,))
    loads["tabs"].wait()

    kinds = ("qu", "vu", "od", "ou")

    def z_copy(m, block, slot, to):
        st, rc = getattr(r, kinds[m] + "s"), getattr(r, kinds[m] + "r")
        return remote(st.at[block], rc.at[slot], r.z_s.at[m, to], r.z_r.at[m, slot], inst=to)

    def stage_kind(m):
        loads[kinds[m]].wait()
        have, st, rc = (getattr(r, kinds[m] + e) for e in "vsr")
        if kinds[m] == "vu":
            st[...] = jnp.zeros_like(st)

        def stage(j):
            block = have[entry(j, SLOTS)]
            if kinds[m] == "vu":
                st[j, :, 0:64] = block
            else:
                st[j] = block

        loop(0, NI, stage)
        rc[i] = st[i]

    def send_kind(m):
        peers(i, NI, lambda p: z_copy(m, p, i, p).start())

    def z_wait(m):
        peers(i, NI, lambda p: z_copy(m, p, p, p).wait_recv())

    for m in range(4):
        stage_kind(m)

    peers(t, NT, lambda p: ss_copy(p, p).wait_recv())
    total = jnp.sum(r.ssb[...], axis=0)
    r.zsb[zc] = jnp.concatenate([total[0:2], old_row, jnp.zeros((5, 128), F32)], axis=0)

    def zs_copy(block, to):
        return remote(
            r.zsb.at[block], r.zsb.at[block], r.zs_s.at[to], r.zs_r.at[block], inst=to * 2 + core
        )

    peers(zc, NZ, lambda p: zs_copy(zc, p).start())
    steps[1]()

    def scales(sums):
        return [
            lax.rsqrt(to_column(sums[s : s + 1, :]) * (1.0 / D) + NORM_EPS) for s in range(2)
        ]

    def normalise(src, scale, gain):
        n0, n1 = (src[s].astype(F32) * scale[s] * gain for s in range(2))
        for p in range(NT):
            rows = slice(8 * p, 8 * p + 8)
            r.nrm[p * OWN : (p + 1) * OWN] = jnp.concatenate(
                [n0[rows], n1[rows]], axis=0
            ).astype(BF16)

    for b in range(NT):
        r.gains[b] = jnp.concatenate([r.ssb[b, 2 + q : 3 + q, :] for q in range(4)], axis=1)
    own_gain = r.gains[t]

    def partial(block):
        sums = r.zsb[block]
        normalise(r.zb.at[block], scales(sums), own_gain)
        slots = to_column(sums[2:3, :]) - (zc * 2 * SLOTS).astype(F32)
        slots = jnp.broadcast_to(slots, (128, 128))
        for p in range(NT):
            for s in range(2):
                lo = p * OWN + s * 8
                r.zmask[lo : lo + 8] = slots[8 * p : 8 * p + 8]
        mask = r.zmask[...]
        rows = r.nrm[...]
        part = jnp.zeros((R2, 128), F32)
        for k in range(SLOTS):
            got = dot(rows, r.dn2[k])
            part = jnp.where(mask == float(k), got[:, :128], part)
            part = jnp.where(mask == float(SLOTS + k), got[:, 128:], part)
        r.ps[:, block] = part.astype(BF16).reshape(NT, OWN, 128)

    load("wq", r.wq, r.wqv)
    r.wkv[...] = jnp.zeros_like(r.wkv)
    lane0 = pl.multiple_of(32 * lax.rem(t, 4), 32)
    load("wk", r.wk, r.wkv.at[pl.ds(lane0, 32)])
    load("wv", r.wv, r.wkv.at[pl.ds(128 + lane0, 32)])
    load("kc", r.kc, r.kext.at[:, pl.ds(0, LMAX)])
    load("vc", r.vc, r.vext.at[:, pl.ds(0, LMAX)])

    zg_pass(1, (1,))
    loads["dn"].wait()
    remote(
        r.dn, r.dn2.at[:, :, pl.ds(half1, 128)], r.dn_s.at[0], r.dn_r.at[0], inst=sibling
    ).wait_recv()
    steps[2]()
    partial(zc)
    zg_pass(2, (0,))
    steps[3]()
    peers(zc, NZ, lambda p: zs_copy(p, p).wait_recv())
    partial(chip(1))
    zg_pass(2, (1,))
    partial(chip(-1))
    def in_order(body, part=slice(None)):
        for dx, dy in WO_ORDER[part]:
            ox, oy = dx + core * (dy - dx), dy + core * (dx - dy)
            body(lax.rem(x + ox, SIDE) * SIDE + lax.rem(y + oy, SIDE))

    def wo_src(p):
        return r.wo.at[pl.ds(core * 128, 128), pl.ds(pl.multiple_of(p * SH, SH), SH)]

    def wo_copy(row, to):
        return remote(wo_src(to), r.wof.at[row, core], r.wo_s.at[to], r.wo_r.at[row], tp=to)

    load("wo", wo_src(t), r.wof.at[t, core])

    def send_wo(n):
        in_order(lambda p: wo_copy(t, p).start(), slice(3 * n, 3 * n + 3))

    zg_pass(3, (0,))
    steps[4]()
    send_wo(0)
    for m in range(2):
        send_kind(m)
    loop(0, 2, lambda k: partial(chip(4 * k - 2)))
    steps[5]()
    send_wo(1)
    zg_pass(3, (1,))
    loop(0, 2, lambda k: partial(chip(6 * k - 3)))
    zg_wait(4, 0)
    zg_wait(4, 1)
    partial(chip(4))

    def pr_copy(block, slot, to):
        return remote(r.ps.at[block], r.pr.at[slot], r.pr_s.at[to], r.pr_r.at[slot], tp=to)

    in_order(lambda p: pr_copy(p, t, p).start())
    r.pr[t] = r.ps[t]
    send_wo(2)
    for ref in (r.qcat, r.vcat, r.oucat, r.qacc, r.kvacc, r.rs2s):
        ref[...] = jnp.zeros_like(ref)
    steps[6]()

    own_scales = scales(total)
    for name in ("wq", "wk", "wv"):
        loads[name].wait()

    def project(b):
        cols = pl.ds(pl.multiple_of(b * SH, SH), SH)
        normalise(r.ag.at[b], own_scales, r.gains[b])
        block = r.nrm[...]
        r.qacc[...] += dot(block, r.wqv[cols, :])
        r.kvacc[...] += dot_nt(block, r.wkv[:, cols])

    loop(0, 6, project)
    peers(t, NT, lambda p: pr_copy(p, p, p).wait_recv())
    sums = jnp.zeros((NZ, OWN, 128), F32)
    for b in range(NT):
        sums += r.pr[b].astype(F32)
    r.rrs[...] = sums.astype(BF16)

    def rr_copy(block, slot, to):
        return remote(
            r.rrs.at[block], r.rr.at[slot], r.rr_s.at[to], r.rr_r.at[slot], inst=to * 2 + core
        )

    peers(zc, NZ, lambda p: rr_copy(p, zc, p).start())
    r.rr[zc] = r.rrs[zc]
    send_wo(3)
    send_kind(2)
    loop(6, 11, project)
    peers(zc, NZ, lambda p: rr_copy(p, p, p).wait_recv())
    r.rk1[t] = jnp.sum(r.rr[...].astype(F32), axis=0).astype(BF16)

    def rk_copy(slot, to):
        return remote(r.rk1.at[slot], r.rk1.at[slot], r.rk1_s.at[to], r.rk1_r.at[slot], tp=to)

    peers(t, NT, lambda p: rk_copy(t, p).start())
    send_wo(4)
    send_kind(3)
    loop(11, NT, project)
    z_wait(0)
    z_wait(1)
    for k in range(SLOTS):
        r.qcat[k * 128 : k * 128 + 64] = r.qur[entry(NI + k, NI)]
        r.vcat[pl.ds(lane0, 32), k * 128 : (k + 1) * 128] = r.vur[entry(NI + k, NI)]
    peers(t, NT, lambda p: rk_copy(p, p).wait_recv())
    rank = r.rk1[...].reshape(R2, 128).astype(F32)
    slot_of_row = r.rmask[...]
    rolled = pltpu.roll(rank, 64, 1)
    for k in range(SLOTS):
        cols = slice(k * 128, (k + 1) * 128)
        r.rall[:, cols] = jnp.where(slot_of_row == float(k), rank, 0.0).astype(BF16)
        r.rall2[:, cols] = jnp.where(slot_of_row == float(k), rolled, 0.0).astype(BF16)

    query = r.qacc[...] + ADAPTER_SCALING * dot(r.rall[...], r.qcat[...])
    fresh_value = r.kvacc[:, 128:] + ADAPTER_SCALING * dot_nt(r.rall2[...], r.vcat[...])
    r.qkvs[:, :, 0:256] = query.astype(BF16).reshape(NT, OWN, 256)
    r.qkvs[:, :, 256:384] = r.kvacc[:, :128].astype(BF16).reshape(NT, OWN, 128)
    r.qkvs[:, :, 384:512] = fresh_value.astype(BF16).reshape(NT, OWN, 128)

    def qkv_copy(block, slot, to):
        return remote(r.qkvs.at[block], r.qkvr.at[slot], r.qkv_s.at[to], r.qkv_r.at[slot], tp=to)

    peers(t, NT, lambda p: qkv_copy(p, t, p).start())
    r.qkvr[t] = r.qkvs[t]

    row = lax.broadcasted_iota(jnp.int32, (OWN, HD), 0)
    lane = lax.broadcasted_iota(jnp.int32, (OWN, HD), 1)
    step_of_row = row // 8
    positions = step_of_row
    for b in range(8):
        positions = positions + jnp.where(lax.rem(row, 8) == b, r.lens[b], 0)
    freq = jnp.exp(lax.rem(lane, 64).astype(F32) * (-math.log(ROPE_BASE) / 64))
    angle = positions.astype(F32) * freq
    cos2 = jnp.cos(angle)
    sin2 = jnp.sin(angle)
    sin2 = jnp.where(lane < 64, -sin2, sin2)

    def rotate(v):
        return v * cos2 + pltpu.roll(v, 64, 1) * sin2

    peers(t, NT, lambda p: ss_copy(p, p).wait_send())
    for c in sent1 + sent_z + [dn_out]:
        c.wait_send()
    peers(zc, NZ, lambda p: zs_copy(p, p).wait_send())
    peers(t, NT, lambda p: pr_copy(p, p, p).wait_send())
    peers(zc, NZ, lambda p: rr_copy(p, p, p).wait_send())
    peers(t, NT, lambda p: rk_copy(p, p).wait_send())
    peers(t, NT, lambda p: qkv_copy(p, p, p).wait_recv())
    loads["kc"].wait()
    loads["vc"].wait()
    for b in range(NT):
        for h in range(2):
            head = r.qkvr[b, :, h * HD : (h + 1) * HD].astype(F32)
            r.q2[pl.ds(2 * b + h, OWN, stride=HEADS)] = rotate(head)
    for g in range(4):
        cols = slice(g * HD, (g + 1) * HD)
        key = jnp.zeros((OWN, HD), F32)
        val = jnp.zeros((OWN, HD), F32)
        for b in range(4 * g, 4 * g + 4):
            key += r.qkvr[b, :, 256:384].astype(F32)
            val += r.qkvr[b, :, 384:512].astype(F32)
        key = rotate(key)
        for b in range(8):
            for v, ref in ((key, r.kext), (val, r.vext)):
                ref[b, LMAX:LPAD, cols] = jnp.where(
                    row == 0, v[b : b + 1], jnp.where(row == 1, v[8 + b : 9 + b], 0.0)
                ).astype(BF16)
    for b in range(8):
        for g in range(4):
            lo = [(s * 8 + b) * HEADS + 8 * g for s in range(2)]
            q = jnp.concatenate([r.q2[o : o + 8] for o in lo], axis=0).astype(BF16)
            score = dot_nt(q, r.kext[b, :, g * HD : (g + 1) * HD])
            r.sc[(b * 4 + g) * OWN : (b * 4 + g + 1) * OWN] = score * (1.0 / math.sqrt(HD))
    at_key = lax.broadcasted_iota(jnp.int32, (64, LPAD), 1)
    at_step = lax.rem(lax.broadcasted_iota(jnp.int32, (64, LPAD), 0) // 8, 2)
    for b in range(8):
        rows = slice(b * 64, (b + 1) * 64)
        live = at_key < jnp.where(at_key < LMAX, r.lens[b], LMAX + 1 + at_step)
        score = jnp.where(live, r.sc[rows], -jnp.inf)
        power = jnp.exp(score - jnp.max(score, axis=1, keepdims=True))
        r.wt[rows] = (power / jnp.sum(power, axis=1, keepdims=True)).astype(BF16)
    for b in range(8):
        for g in range(4):
            weight = r.wt[(b * 4 + g) * OWN : (b * 4 + g + 1) * OWN]
            mix = dot(weight, r.vext[b, :, g * HD : (g + 1) * HD])
            for s in range(2):
                lo = (s * 8 + b) * HEADS + 8 * g
                r.o2[lo : lo + 8] = mix[s * 8 : s * 8 + 8]
    for h in range(HEADS):
        r.ag2[t, :, h * HD : (h + 1) * HD] = r.o2[pl.ds(h, OWN, stride=HEADS)].astype(BF16)

    def at_copy(cols_of, slot, to):
        src = r.ag2.at[t, :, pl.ds(pl.multiple_of(cols_of * 256, 256), 256)]
        return remote(src, r.attd.at[slot], r.at_s.at[to], r.at_r.at[slot], tp=to)

    peers(t, NT, lambda p: at_copy(p, t, p).start())

    def ag2_ref(block, p, half):
        if half is None:
            return r.ag2.at[block, :, pl.ds(p * 2048, 2048)]
        return r.ag2.at[block, :, pl.ds(p * 2048 + half * 1024, 1024)]

    start, steps, sent2 = mesh_gather(x, y, ag2_ref, r.ag2_s, r.ag2_r)
    start()
    r.attd[t] = r.ag2[t, :, pl.ds(pl.multiple_of(t * 256, 256), 256)]
    steps[0]()
    z_wait(2)
    peers(t, NT, lambda p: at_copy(p, p, p).wait_recv())
    heads = r.attd[...].reshape(R2, 256)
    part = jnp.zeros((R2, 64), F32)
    for k in range(SLOTS):
        got = dot_nt(heads, r.odr[entry(NI + k, NI)])
        part = jnp.where(slot_of_row[:, :64] == float(k), got, part)
    r.rs2s[:, :, 0:64] = part.reshape(NT, OWN, 64)

    def c1(block, slot, to):
        return remote(r.rs2s.at[block], r.rs2r.at[slot], r.rs2_s.at[to], r.rs2_r.at[slot], tp=to)

    def c2(slot, to):
        return remote(r.rk2.at[slot], r.rk2.at[slot], r.rk2_s.at[to], r.rk2_r.at[slot], tp=to)

    peers(t, NT, lambda p: c1(p, t, p).start())
    r.rs2r[t] = r.rs2s[t]
    steps[1]()
    steps[2]()
    loads["wo"].wait()
    peers(t, NT, lambda p: wo_copy(p, p).wait_recv())
    sib = remote(
        r.wof.at[:, core], r.wof.at[:, core], r.sib_s.at[0], r.sib_r.at[0], inst=sibling
    )
    sib.start()
    peers(t, NT, lambda p: c1(p, p, p).wait_recv())
    r.rk2[t] = jnp.sum(r.rs2r[...], axis=0).astype(BF16)
    peers(t, NT, lambda p: c2(t, p).start())
    peers(t, NT, lambda p: qkv_copy(p, p, p).wait_send())
    peers(t, NT, lambda p: wo_copy(p, p).wait_send())
    for m in range(3):
        peers(i, NI, lambda p, m=m: z_copy(m, p, p, p).wait_send())
    for step in steps[3:]:
        step()

    sib_in = remote(
        r.wof.at[:, 1 - core], r.wof.at[:, 1 - core], r.sib_s.at[0], r.sib_r.at[0], inst=sibling
    )
    sib_in.wait_recv()
    r.oacc[...] = jnp.zeros_like(r.oacc)

    def out_chunk(c):
        lhs = r.ag2[:, :, pl.ds(pl.multiple_of(c * 512, 512), 512)].reshape(R2, 512)
        rhs = r.wof[pl.ds(c * 2, 2)].reshape(512, SH)
        r.oacc[...] += dot(lhs, rhs)

    loop(0, 8, out_chunk)
    peers(t, NT, lambda p: c2(p, p).wait_recv())
    rank = r.rk2[...].reshape(R2, 128).astype(F32)
    for k in range(SLOTS):
        cols = slice(k * 128, (k + 1) * 128)
        r.rall[:, cols] = jnp.where(slot_of_row == float(k), rank, 0.0).astype(BF16)
    z_wait(3)
    for k in range(SLOTS):
        r.oucat[k * 128 : k * 128 + 64] = r.our[entry(NI + k, NI)]
    res = r.oacc[...] + ADAPTER_SCALING * dot(r.rall[...], r.oucat[...])
    for p in range(NT):
        for s in range(2):
            lo = p * OWN + s * 8
            r.oacc[s * ROWS + p * 8 : s * ROWS + p * 8 + 8] = res[lo : lo + 8]
    for s in range(2):
        r.out[s] = r.oacc[s * ROWS : (s + 1) * ROWS].astype(BF16)

    for c in sent2:
        c.wait_send()
    peers(i, NI, lambda p: z_copy(3, p, p, p).wait_send())
    sib.wait_send()
    peers(t, NT, lambda p: at_copy(p, p, p).wait_send())
    peers(t, NT, lambda p: c1(p, p, p).wait_send())
    peers(t, NT, lambda p: c2(p, p).wait_send())


def local(
    hidden_in,
    norm_gain,
    query_weight,
    w_key,
    value_weight,
    w_output,
    paired_down_matrices,
    query_up_matrices,
    value_up_matrices,
    output_down_matrices,
    output_up_matrices,
    key_cache,
    value_cache,
    cache_lengths,
    row_adapter,
    old_slot,
    new_slot,
):
    smem = pl.BlockSpec(memory_space=pltpu.SMEM)
    vmem = pl.BlockSpec(memory_space=pltpu.VMEM)
    hbm = pl.BlockSpec(memory_space=pl.ANY)
    return pl.pallas_call(
        kernel,
        out_shape=jax.ShapeDtypeStruct((2, ROWS, SH), BF16),
        in_specs=[smem] + [vmem] * 4 + [hbm] * 12,
        out_specs=vmem,
        scratch_shapes=[pltpu.SMEM((8, 128), jnp.int32)]
        + [pltpu.VMEM(*s) for s in SCRATCH.values()]
        + [pltpu.SemaphoreType.DMA(s) for s in SEMS.values()],
        compiler_params=pltpu.CompilerParams(
            collective_id=0, has_side_effects=True, vmem_limit_bytes=58 * 2**20
        ),
        name="decode_block",
    )(
        cache_lengths,
        norm_gain.reshape(4, 128),
        row_adapter.reshape(1, ROWS),
        old_slot.reshape(1, -1),
        new_slot.reshape(1, -1),
        hidden_in,
        query_weight,
        w_key.T,
        value_weight.T,
        w_output,
        paired_down_matrices,
        query_up_matrices,
        jnp.swapaxes(value_up_matrices, 1, 2),
        output_down_matrices,
        output_up_matrices,
        key_cache,
        value_cache,
    )


def solution(mesh):
    placed = (
        P(None, "inst", "tp"),
        P("tp"),
        P(None, "tp"),
        P(None, "tp"),
        P(None, "tp"),
        P("tp", None),
        P("inst", "tp", None),
        P("inst", None, "tp"),
        P("inst", None, "tp"),
        P("inst", None, "tp"),
        P("inst", None, "tp"),
        P(("inst", "tp"), None, None),
        P(("inst", "tp"), None, None),
        P(("inst", "tp")),
        P("inst"),
        P(),
        P(),
    )
    return jax.shard_map(
        local, mesh=mesh, in_specs=placed, out_specs=P(None, "inst", "tp"), check_vma=False
    )
```

```python
import functools
import math

import jax
import jax.numpy as jnp
from jax import lax
from jax.experimental import pallas as pl
from jax.experimental.pallas import tpu as pltpu
from jax.sharding import PartitionSpec as P

MESH = pl.DeviceIdType.MESH
F32, BF16 = jnp.float32, jnp.bfloat16

NT = 16
NI = 16
NZ = 8
SIDE = 4
D = 8192
SH = 512
ROWS = 128
R2 = 256
OWN = 16
HEADS = 32
HD = 128
SLOTS = 8
LMAX = 64
LPAD = 80
ADAPTER_SCALING = 0.5
NORM_EPS = 1e-05
ROPE_BASE = 500000.0

WO_ORDER = (
    (1, 0), (0, 3), (3, 0), (0, 1), (1, 1), (3, 3), (1, 3), (3, 1),
    (2, 0), (0, 2), (2, 1), (1, 2), (2, 3), (3, 2), (2, 2),
)

SCRATCH = dict(
    tabv=((8, 128), jnp.int32),
    rmask=((R2, 128), F32),
    ag=((NT, 2, ROWS, SH), BF16),
    nrm=((R2, SH), BF16),
    gains=((NT, 1, SH), F32),
    sc=((8 * 64, LPAD), F32),
    wt=((8 * 64, LPAD), BF16),
    wqv=((D, 256), BF16),
    wkv=((256, D), BF16),
    wof=((NT, 2, 128, SH), BF16),
    dn2=((SLOTS, SH, 256), BF16),
    zb=((NZ, 2, ROWS, SH), BF16),
    zsb=((NZ, 8, 128), F32),
    zmask=((R2, 128), F32),
    ps=((NT, NZ, OWN, 128), BF16),
    pr=((NT, NZ, OWN, 128), BF16),
    rrs=((NZ, OWN, 128), BF16),
    rr=((NZ, OWN, 128), BF16),
    quv=((SLOTS, 64, 256), BF16),
    vuv=((SLOTS, 32, 64), BF16),
    odv=((SLOTS, 64, 256), BF16),
    ouv=((SLOTS, 64, SH), BF16),
    qus=((NI, 64, 256), BF16),
    vus=((NI, 32, 128), BF16),
    ods=((NI, 64, 256), BF16),
    ous=((NI, 64, SH), BF16),
    qur=((NI, 64, 256), BF16),
    vur=((NI, 32, 128), BF16),
    odr=((NI, 64, 256), BF16),
    our=((NI, 64, SH), BF16),
    qcat=((SLOTS * 128, 256), BF16),
    vcat=((128, SLOTS * 128), BF16),
    oucat=((SLOTS * 128, SH), BF16),
    rall=((R2, SLOTS * 128), BF16),
    rall2=((R2, SLOTS * 128), BF16),
    kext=((8, LPAD, 512), BF16),
    vext=((8, LPAD, 512), BF16),
    ssb=((NT, 8, 128), F32),
    rk1=((NT, OWN, 128), BF16),
    rs2s=((NT, OWN, 128), F32),
    rs2r=((NT, OWN, 128), F32),
    rk2=((NT, OWN, 128), BF16),
    qacc=((R2, 256), F32),
    kvacc=((R2, 256), F32),
    qkvs=((NT, OWN, 512), BF16),
    qkvr=((NT, OWN, 512), BF16),
    q2=((OWN * HEADS, HD), F32),
    o2=((OWN * HEADS, HD), F32),
    ag2=((NT, OWN, HEADS * HD), BF16),
    attd=((NT, OWN, 256), BF16),
    oacc=((R2, SH), F32),
)
SEMS = dict(
    ld=(16,),
    ss_s=(NT,), ss_r=(NT,),
    ag_s=(2, 20), ag_r=(2, NT, 2),
    z_s=(4, NI), z_r=(4, NI),
    zg_s=(14,), zg_r=(NZ, 2), zs_s=(NZ,), zs_r=(NZ,), dn_s=(1,), dn_r=(1,),
    pr_s=(NT,), pr_r=(NT,), rr_s=(NZ,), rr_r=(NZ,),
    wo_s=(NT,), wo_r=(NT,), sib_s=(1,), sib_r=(1,),
    rk1_s=(NT,), rk1_r=(NT,),
    qkv_s=(NT,), qkv_r=(NT,),
    ag2_s=(2, 20), ag2_r=(2, NT, 2),
    at_s=(NT,), at_r=(NT,),
    rs2_s=(NT,), rs2_r=(NT,), rk2_s=(NT,), rk2_r=(NT,),
)
INPUTS = (
    "lens", "gain", "adapter", "old", "new", "hid", "wq", "wk", "wv", "wo",
    "dn", "qu", "vu", "od", "ou", "kc", "vc",
)


class Refs:
    pass


def dot(a, b):
    return lax.dot_general(a, b, (((1,), (0,)), ((), ())), preferred_element_type=F32)


def dot_nt(a, b):
    return lax.dot_general(a, b, (((1,), (1,)), ((), ())), preferred_element_type=F32)


def remote(src, dst, ssem, rsem, **where):
    return pltpu.make_async_remote_copy(
        src_ref=src, dst_ref=dst, send_sem=ssem, recv_sem=rsem, device_id=where, device_id_type=MESH
    )


def loop(lo, hi, body):
    lax.fori_loop(lo, hi, lambda k, c: (body(k), c)[1], 0)


def peers(me, n, body):
    loop(1, n, lambda k: body(lax.rem(me + k, n)))


def mesh_gather(x, y, ref_of, ssem, rsem):
    def at(p, da, db):
        ax, ay = (da, db) if p == 0 else (db, da)
        return lax.rem(x + ax + SIDE, SIDE) * SIDE + lax.rem(y + ay + SIDE, SIDE)

    count = [0, 0]
    sent = []

    def copy(p, da, db, half, to, idx):
        block = at(p, da, db)
        ref = ref_of(block, p, half)
        return remote(
            ref, ref, ssem.at[p, idx], rsem.at[p, block, half or 0], tp=at(p, *to)
        )

    def send(p, da, db, half, to):
        c = copy(p, da, db, half, to, count[p])
        count[p] += 1
        c.start()
        sent.append(c)

    def wait(p, da, db, half=None):
        copy(p, da, db, half, (1, 0), 0).wait_recv()

    def start():
        for p in range(2):
            for to in ((1, 0), (-1, 0), (0, 1), (0, -1)):
                send(p, 0, 0, None, to)

    def along_b(p, da):
        send(p, da, 0, None, (0, 1))
        send(p, da, 0, None, (0, -1))

    def s1():
        for p in range(2):
            wait(p, -1, 0)
            send(p, -1, 0, 0, (1, 0))
            along_b(p, -1)
        for p in range(2):
            wait(p, 1, 0)
            send(p, 1, 0, 1, (-1, 0))
            along_b(p, 1)

    def s2():
        for p in range(2):
            wait(p, 0, -1)
            send(p, 0, -1, 0, (0, 1))
            wait(p, 0, 1)
            send(p, 0, 1, 1, (0, -1))

    def s3():
        for p in range(2):
            wait(p, 2, 0, 0)
            wait(p, 2, 0, 1)
            along_b(p, 2)

    def s4():
        for da in (-1, 1):
            for p in range(2):
                wait(p, da, -1)
                send(p, da, -1, 0, (0, 1))
                wait(p, da, 1)
                send(p, da, 1, 1, (0, -1))

    def s5():
        for p in range(2):
            wait(p, 0, 2, 0)
            wait(p, 0, 2, 1)

    def s6():
        for p in range(2):
            wait(p, 2, -1)
            send(p, 2, -1, 0, (0, 1))
            wait(p, 2, 1)
            send(p, 2, 1, 1, (0, -1))

    def s7():
        for da in (-1, 1, 2):
            for p in range(2):
                wait(p, da, 2, 0)
                wait(p, da, 2, 1)

    return start, (s1, s2, s3, s4, s5, s6, s7), sent


def kernel(*args):
    names = list(INPUTS) + ["out", "tabs"] + list(SCRATCH) + list(SEMS)
    r = Refs()
    for name, ref in zip(names, args, strict=True):
        setattr(r, name, ref)
    i = lax.axis_index("inst")
    t = lax.axis_index("tp")
    x, y = t // SIDE, lax.rem(t, SIDE)
    core = lax.rem(i, 2)
    zc = i // 2
    sibling = i + 1 - 2 * core

    loads = {}

    def load(name, src, dst):
        c = pltpu.make_async_copy(src, dst, r.ld.at[len(loads)])
        c.start()
        loads[name] = c

    load("hid", r.hid, r.ag.at[t])
    half0 = pl.multiple_of(core * 128, 128)
    half1 = pl.multiple_of(128 - core * 128, 128)
    load("dn", r.dn, r.dn2.at[:, :, pl.ds(half0, 128)])
    for m in ("qu", "vu", "od", "ou"):
        load(m, getattr(r, m), getattr(r, m + "v"))

    bar = pltpu.get_barrier_semaphore()

    def hello(axis, p):
        pl.semaphore_signal(bar, inc=1, device_id={axis: p}, device_id_type=MESH)

    peers(t, NT, lambda p: hello("tp", p))
    peers(i, NI, lambda p: hello("inst", p))

    loads["hid"].wait()
    pl.semaphore_wait(bar, NT + NI - 2)

    def ag_ref(block, p, half):
        if half is None:
            return r.ag.at[block, p]
        return r.ag.at[block, p, pl.ds(half * 64, 64)]

    start, steps, sent1 = mesh_gather(x, y, ag_ref, r.ag_s, r.ag_r)
    start()

    def chip(d):
        return lax.rem(zc + d + NZ, NZ)

    def zg_copy(d, half, to, idx):
        block = chip(d)
        src, dst = (r.ag.at[t] if d == 0 else r.zb.at[block]), r.zb.at[block]
        if half is not None:
            src, dst = src.at[half], dst.at[half]
        return remote(
            src, dst, r.zg_s.at[idx], r.zg_r.at[block, half or 0], inst=chip(to) * 2 + core
        )

    sent_z = []

    def zg_send(*what):
        c = zg_copy(*what, len(sent_z))
        c.start()
        sent_z.append(c)

    def zg_wait(d, half=None):
        zg_copy(d, half, 1, 0).wait_recv()

    def zg_pass(d, order):
        for n in order:
            for side in (-1, 1):
                half = n if side < 0 else 1 - n
                zg_wait(side * d, half)
                if d < 3 or n == 0:
                    zg_send(side * d, half, -side)

    for n in range(2):
        zg_send(0, n, 1)
        zg_send(0, 1 - n, -1)
    dn_out = remote(
        r.dn, r.dn2.at[:, :, pl.ds(half0, 128)], r.dn_s.at[0], r.dn_r.at[0], inst=sibling
    )
    dn_out.start()
    r.zb[zc] = r.ag[t]
    sub = lax.broadcasted_iota(jnp.int32, (128, 128), 0)
    lan = lax.broadcasted_iota(jnp.int32, (128, 128), 1)
    eye = sub == lan

    def to_column(v):
        return jnp.sum(jnp.where(eye, v, 0.0), axis=1, keepdims=True)

    def to_row(v):
        return jnp.sum(jnp.where(eye, v, 0.0), axis=0, keepdims=True)

    parts = []
    for s in range(2):
        h = r.ag[t, s].astype(F32)
        parts.append(to_row(jnp.sum(h * h, axis=1, keepdims=True)))
    gain = r.gain[...].astype(F32)
    r.ssb[t] = jnp.concatenate(parts + [gain, jnp.zeros((2, 128), F32)], axis=0)

    def ss_copy(src_block, to):
        return remote(
            r.ssb.at[src_block], r.ssb.at[src_block], r.ss_s.at[to], r.ss_r.at[src_block], tp=to
        )

    peers(t, NT, lambda p: ss_copy(t, p).start())


    old, new = r.old[...], r.new[...]
    goes = ((old >> 3) == i) & ((new >> 3) == sub) & (sub < NI)
    comes = (new == i * SLOTS + sub - NI) & (sub >= NI) & (sub < NI + SLOTS)
    table = jnp.where(goes, old & 7, 0) + jnp.where(comes, old >> 3, 0)
    table = jnp.sum(table, axis=1, keepdims=True)
    table = jnp.sum(jnp.where(eye, table, 0), axis=0, keepdims=True)
    r.tabv[...] = jnp.broadcast_to(table, (8, 128))
    load("tabs", r.tabv, r.tabs)
    named = to_column(r.adapter[...].astype(F32)) == lan.astype(F32)
    slot_column = jnp.sum(jnp.where(named, new.astype(F32), 0.0), axis=1, keepdims=True)
    old_row = to_row(
        jnp.sum(jnp.where(named, old.astype(F32), 0.0), axis=1, keepdims=True)
    )
    slot_column = jnp.broadcast_to(slot_column - (i * SLOTS).astype(F32), (128, 128))
    for p in range(NT):
        for s in range(2):
            r.rmask[p * OWN + s * 8 : p * OWN + s * 8 + 8] = slot_column[8 * p : 8 * p + 8]

    def entry(n, top):
        return jnp.clip(r.tabs[0, n], 0, top - 1)

    steps[0]()
    zg_pass(1, (0,))
    loads["tabs"].wait()

    kinds = ("qu", "vu", "od", "ou")

    def z_copy(m, block, slot, to):
        st, rc = getattr(r, kinds[m] + "s"), getattr(r, kinds[m] + "r")
        return remote(st.at[block], rc.at[slot], r.z_s.at[m, to], r.z_r.at[m, slot], inst=to)

    def stage_kind(m):
        loads[kinds[m]].wait()
        have, st, rc = (getattr(r, kinds[m] + e) for e in "vsr")
        if kinds[m] == "vu":
            st[...] = jnp.zeros_like(st)

        def stage(j):
            block = have[entry(j, SLOTS)]
            if kinds[m] == "vu":
                st[j, :, 0:64] = block
            else:
                st[j] = block

        loop(0, NI, stage)
        rc[i] = st[i]

    def send_kind(m):
        peers(i, NI, lambda p: z_copy(m, p, i, p).start())

    def z_wait(m):
        peers(i, NI, lambda p: z_copy(m, p, p, p).wait_recv())

    for m in range(4):
        stage_kind(m)

    peers(t, NT, lambda p: ss_copy(p, p).wait_recv())
    total = jnp.sum(r.ssb[...], axis=0)
    r.zsb[zc] = jnp.concatenate([total[0:2], old_row, jnp.zeros((5, 128), F32)], axis=0)

    def zs_copy(block, to):
        return remote(
            r.zsb.at[block], r.zsb.at[block], r.zs_s.at[to], r.zs_r.at[block], inst=to * 2 + core
        )

    peers(zc, NZ, lambda p: zs_copy(zc, p).start())
    steps[1]()

    def scales(sums):
        return [
            lax.rsqrt(to_column(sums[s : s + 1, :]) * (1.0 / D) + NORM_EPS) for s in range(2)
        ]

    def normalise(src, scale, gain):
        n0, n1 = (src[s].astype(F32) * scale[s] * gain for s in range(2))
        for p in range(NT):
            rows = slice(8 * p, 8 * p + 8)
            r.nrm[p * OWN : (p + 1) * OWN] = jnp.concatenate(
                [n0[rows], n1[rows]], axis=0
            ).astype(BF16)

    for b in range(NT):
        r.gains[b] = jnp.concatenate([r.ssb[b, 2 + q : 3 + q, :] for q in range(4)], axis=1)
    own_gain = r.gains[t]

    def partial(block):
        sums = r.zsb[block]
        normalise(r.zb.at[block], scales(sums), own_gain)
        slots = to_column(sums[2:3, :]) - (zc * 2 * SLOTS).astype(F32)
        slots = jnp.broadcast_to(slots, (128, 128))
        for p in range(NT):
            for s in range(2):
                lo = p * OWN + s * 8
                r.zmask[lo : lo + 8] = slots[8 * p : 8 * p + 8]
        mask = r.zmask[...]
        rows = r.nrm[...]
        part = jnp.zeros((R2, 128), F32)
        for k in range(SLOTS):
            got = dot(rows, r.dn2[k])
            part = jnp.where(mask == float(k), got[:, :128], part)
            part = jnp.where(mask == float(SLOTS + k), got[:, 128:], part)
        r.ps[:, block] = part.astype(BF16).reshape(NT, OWN, 128)

    load("wq", r.wq, r.wqv)
    r.wkv[...] = jnp.zeros_like(r.wkv)
    lane0 = pl.multiple_of(32 * lax.rem(t, 4), 32)
    load("wk", r.wk, r.wkv.at[pl.ds(lane0, 32)])
    load("wv", r.wv, r.wkv.at[pl.ds(128 + lane0, 32)])
    load("kc", r.kc, r.kext.at[:, pl.ds(0, LMAX)])
    load("vc", r.vc, r.vext.at[:, pl.ds(0, LMAX)])

    zg_pass(1, (1,))
    loads["dn"].wait()
    remote(
        r.dn, r.dn2.at[:, :, pl.ds(half1, 128)], r.dn_s.at[0], r.dn_r.at[0], inst=sibling
    ).wait_recv()
    steps[2]()
    partial(zc)
    zg_pass(2, (0,))
    steps[3]()
    peers(zc, NZ, lambda p: zs_copy(p, p).wait_recv())
    partial(chip(1))
    zg_pass(2, (1,))
    partial(chip(-1))
    def in_order(body, part=slice(None)):
        for dx, dy in WO_ORDER[part]:
            ox, oy = dx + core * (dy - dx), dy + core * (dx - dy)
            body(lax.rem(x + ox, SIDE) * SIDE + lax.rem(y + oy, SIDE))

    def wo_src(p):
        return r.wo.at[pl.ds(core * 128, 128), pl.ds(pl.multiple_of(p * SH, SH), SH)]

    def wo_copy(row, to):
        return remote(wo_src(to), r.wof.at[row, core], r.wo_s.at[to], r.wo_r.at[row], tp=to)

    load("wo", wo_src(t), r.wof.at[t, core])

    def send_wo(n):
        in_order(lambda p: wo_copy(t, p).start(), slice(3 * n, 3 * n + 3))

    zg_pass(3, (0,))
    steps[4]()
    send_wo(0)
    for m in range(2):
        send_kind(m)
    loop(0, 2, lambda k: partial(chip(4 * k - 2)))
    steps[5]()
    send_wo(1)
    zg_pass(3, (1,))
    loop(0, 2, lambda k: partial(chip(6 * k - 3)))
    zg_wait(4, 0)
    zg_wait(4, 1)
    partial(chip(4))

    def pr_copy(block, slot, to):
        return remote(r.ps.at[block], r.pr.at[slot], r.pr_s.at[to], r.pr_r.at[slot], tp=to)

    in_order(lambda p: pr_copy(p, t, p).start())
    r.pr[t] = r.ps[t]
    send_wo(2)
    for ref in (r.qcat, r.vcat, r.oucat, r.qacc, r.kvacc, r.rs2s):
        ref[...] = jnp.zeros_like(ref)
    steps[6]()

    own_scales = scales(total)
    for name in ("wq", "wk", "wv"):
        loads[name].wait()

    def project(b):
        cols = pl.ds(pl.multiple_of(b * SH, SH), SH)
        normalise(r.ag.at[b], own_scales, r.gains[b])
        block = r.nrm[...]
        r.qacc[...] += dot(block, r.wqv[cols, :])
        r.kvacc[...] += dot_nt(block, r.wkv[:, cols])

    loop(0, 6, project)
    peers(t, NT, lambda p: pr_copy(p, p, p).wait_recv())
    sums = jnp.zeros((NZ, OWN, 128), F32)
    for b in range(NT):
        sums += r.pr[b].astype(F32)
    r.rrs[...] = sums.astype(BF16)

    def rr_copy(block, slot, to):
        return remote(
            r.rrs.at[block], r.rr.at[slot], r.rr_s.at[to], r.rr_r.at[slot], inst=to * 2 + core
        )

    peers(zc, NZ, lambda p: rr_copy(p, zc, p).start())
    r.rr[zc] = r.rrs[zc]
    send_wo(3)
    loop(6, 11, project)
    peers(zc, NZ, lambda p: rr_copy(p, p, p).wait_recv())
    r.rk1[t] = jnp.sum(r.rr[...].astype(F32), axis=0).astype(BF16)

    def rk_copy(slot, to):
        return remote(r.rk1.at[slot], r.rk1.at[slot], r.rk1_s.at[to], r.rk1_r.at[slot], tp=to)

    peers(t, NT, lambda p: rk_copy(t, p).start())
    send_wo(4)
    send_kind(2)
    send_kind(3)
    loop(11, NT, project)
    z_wait(0)
    z_wait(1)
    for k in range(SLOTS):
        r.qcat[k * 128 : k * 128 + 64] = r.qur[entry(NI + k, NI)]
        r.vcat[pl.ds(lane0, 32), k * 128 : (k + 1) * 128] = r.vur[entry(NI + k, NI)]
    peers(t, NT, lambda p: rk_copy(p, p).wait_recv())
    rank = r.rk1[...].reshape(R2, 128).astype(F32)
    slot_of_row = r.rmask[...]
    rolled = pltpu.roll(rank, 64, 1)
    for k in range(SLOTS):
        cols = slice(k * 128, (k + 1) * 128)
        r.rall[:, cols] = jnp.where(slot_of_row == float(k), rank, 0.0).astype(BF16)
        r.rall2[:, cols] = jnp.where(slot_of_row == float(k), rolled, 0.0).astype(BF16)

    query = r.qacc[...] + ADAPTER_SCALING * dot(r.rall[...], r.qcat[...])
    fresh_value = r.kvacc[:, 128:] + ADAPTER_SCALING * dot_nt(r.rall2[...], r.vcat[...])
    r.qkvs[:, :, 0:256] = query.astype(BF16).reshape(NT, OWN, 256)
    r.qkvs[:, :, 256:384] = r.kvacc[:, :128].astype(BF16).reshape(NT, OWN, 128)
    r.qkvs[:, :, 384:512] = fresh_value.astype(BF16).reshape(NT, OWN, 128)

    def qkv_copy(block, slot, to):
        return remote(r.qkvs.at[block], r.qkvr.at[slot], r.qkv_s.at[to], r.qkv_r.at[slot], tp=to)

    peers(t, NT, lambda p: qkv_copy(p, t, p).start())
    r.qkvr[t] = r.qkvs[t]

    row = lax.broadcasted_iota(jnp.int32, (OWN, HD), 0)
    lane = lax.broadcasted_iota(jnp.int32, (OWN, HD), 1)
    step_of_row = row // 8
    positions = step_of_row
    for b in range(8):
        positions = positions + jnp.where(lax.rem(row, 8) == b, r.lens[b], 0)
    freq = jnp.exp(lax.rem(lane, 64).astype(F32) * (-math.log(ROPE_BASE) / 64))
    angle = positions.astype(F32) * freq
    cos2 = jnp.cos(angle)
    sin2 = jnp.sin(angle)
    sin2 = jnp.where(lane < 64, -sin2, sin2)

    def rotate(v):
        return v * cos2 + pltpu.roll(v, 64, 1) * sin2

    peers(t, NT, lambda p: ss_copy(p, p).wait_send())
    for c in sent1 + sent_z + [dn_out]:
        c.wait_send()
    peers(zc, NZ, lambda p: zs_copy(p, p).wait_send())
    peers(t, NT, lambda p: pr_copy(p, p, p).wait_send())
    peers(zc, NZ, lambda p: rr_copy(p, p, p).wait_send())
    peers(t, NT, lambda p: rk_copy(p, p).wait_send())
    peers(t, NT, lambda p: qkv_copy(p, p, p).wait_recv())
    loads["kc"].wait()
    loads["vc"].wait()
    for b in range(NT):
        for h in range(2):
            head = r.qkvr[b, :, h * HD : (h + 1) * HD].astype(F32)
            r.q2[pl.ds(2 * b + h, OWN, stride=HEADS)] = rotate(head)
    for g in range(4):
        cols = slice(g * HD, (g + 1) * HD)
        key = jnp.zeros((OWN, HD), F32)
        val = jnp.zeros((OWN, HD), F32)
        for b in range(4 * g, 4 * g + 4):
            key += r.qkvr[b, :, 256:384].astype(F32)
            val += r.qkvr[b, :, 384:512].astype(F32)
        key = rotate(key)
        for b in range(8):
            for v, ref in ((key, r.kext), (val, r.vext)):
                ref[b, LMAX:LPAD, cols] = jnp.where(
                    row == 0, v[b : b + 1], jnp.where(row == 1, v[8 + b : 9 + b], 0.0)
                ).astype(BF16)
    for b in range(8):
        for g in range(4):
            lo = [(s * 8 + b) * HEADS + 8 * g for s in range(2)]
            q = jnp.concatenate([r.q2[o : o + 8] for o in lo], axis=0).astype(BF16)
            score = dot_nt(q, r.kext[b, :, g * HD : (g + 1) * HD])
            r.sc[(b * 4 + g) * OWN : (b * 4 + g + 1) * OWN] = score * (1.0 / math.sqrt(HD))
    at_key = lax.broadcasted_iota(jnp.int32, (64, LPAD), 1)
    at_step = lax.rem(lax.broadcasted_iota(jnp.int32, (64, LPAD), 0) // 8, 2)
    for b in range(8):
        rows = slice(b * 64, (b + 1) * 64)
        live = at_key < jnp.where(at_key < LMAX, r.lens[b], LMAX + 1 + at_step)
        score = jnp.where(live, r.sc[rows], -jnp.inf)
        power = jnp.exp(score - jnp.max(score, axis=1, keepdims=True))
        r.wt[rows] = (power / jnp.sum(power, axis=1, keepdims=True)).astype(BF16)
    for b in range(8):
        for g in range(4):
            weight = r.wt[(b * 4 + g) * OWN : (b * 4 + g + 1) * OWN]
            mix = dot(weight, r.vext[b, :, g * HD : (g + 1) * HD])
            for s in range(2):
                lo = (s * 8 + b) * HEADS + 8 * g
                r.o2[lo : lo + 8] = mix[s * 8 : s * 8 + 8]
    for h in range(HEADS):
        r.ag2[t, :, h * HD : (h + 1) * HD] = r.o2[pl.ds(h, OWN, stride=HEADS)].astype(BF16)

    def at_copy(cols_of, slot, to):
        src = r.ag2.at[t, :, pl.ds(pl.multiple_of(cols_of * 256, 256), 256)]
        return remote(src, r.attd.at[slot], r.at_s.at[to], r.at_r.at[slot], tp=to)

    peers(t, NT, lambda p: at_copy(p, t, p).start())

    def ag2_ref(block, p, half):
        if half is None:
            return r.ag2.at[block, :, pl.ds(p * 2048, 2048)]
        return r.ag2.at[block, :, pl.ds(p * 2048 + half * 1024, 1024)]

    start, steps, sent2 = mesh_gather(x, y, ag2_ref, r.ag2_s, r.ag2_r)
    start()
    r.attd[t] = r.ag2[t, :, pl.ds(pl.multiple_of(t * 256, 256), 256)]
    steps[0]()
    z_wait(2)
    peers(t, NT, lambda p: at_copy(p, p, p).wait_recv())
    heads = r.attd[...].reshape(R2, 256)
    part = jnp.zeros((R2, 64), F32)
    for k in range(SLOTS):
        got = dot_nt(heads, r.odr[entry(NI + k, NI)])
        part = jnp.where(slot_of_row[:, :64] == float(k), got, part)
    r.rs2s[:, :, 0:64] = part.reshape(NT, OWN, 64)

    def c1(block, slot, to):
        return remote(r.rs2s.at[block], r.rs2r.at[slot], r.rs2_s.at[to], r.rs2_r.at[slot], tp=to)

    def c2(slot, to):
        return remote(r.rk2.at[slot], r.rk2.at[slot], r.rk2_s.at[to], r.rk2_r.at[slot], tp=to)

    peers(t, NT, lambda p: c1(p, t, p).start())
    r.rs2r[t] = r.rs2s[t]
    steps[1]()
    steps[2]()
    loads["wo"].wait()
    peers(t, NT, lambda p: wo_copy(p, p).wait_recv())
    sib = remote(
        r.wof.at[:, core], r.wof.at[:, core], r.sib_s.at[0], r.sib_r.at[0], inst=sibling
    )
    sib.start()
    peers(t, NT, lambda p: c1(p, p, p).wait_recv())
    r.rk2[t] = jnp.sum(r.rs2r[...], axis=0).astype(BF16)
    peers(t, NT, lambda p: c2(t, p).start())
    peers(t, NT, lambda p: qkv_copy(p, p, p).wait_send())
    peers(t, NT, lambda p: wo_copy(p, p).wait_send())
    for m in range(3):
        peers(i, NI, lambda p, m=m: z_copy(m, p, p, p).wait_send())
    for step in steps[3:]:
        step()

    sib_in = remote(
        r.wof.at[:, 1 - core], r.wof.at[:, 1 - core], r.sib_s.at[0], r.sib_r.at[0], inst=sibling
    )
    sib_in.wait_recv()
    r.oacc[...] = jnp.zeros_like(r.oacc)

    def out_chunk(c):
        lhs = r.ag2[:, :, pl.ds(pl.multiple_of(c * 512, 512), 512)].reshape(R2, 512)
        rhs = r.wof[pl.ds(c * 2, 2)].reshape(512, SH)
        r.oacc[...] += dot(lhs, rhs)

    loop(0, 8, out_chunk)
    peers(t, NT, lambda p: c2(p, p).wait_recv())
    rank = r.rk2[...].reshape(R2, 128).astype(F32)
    for k in range(SLOTS):
        cols = slice(k * 128, (k + 1) * 128)
        r.rall[:, cols] = jnp.where(slot_of_row == float(k), rank, 0.0).astype(BF16)
    z_wait(3)
    for k in range(SLOTS):
        r.oucat[k * 128 : k * 128 + 64] = r.our[entry(NI + k, NI)]
    res = r.oacc[...] + ADAPTER_SCALING * dot(r.rall[...], r.oucat[...])
    for p in range(NT):
        for s in range(2):
            lo = p * OWN + s * 8
            r.oacc[s * ROWS + p * 8 : s * ROWS + p * 8 + 8] = res[lo : lo + 8]
    for s in range(2):
        r.out[s] = r.oacc[s * ROWS : (s + 1) * ROWS].astype(BF16)

    for c in sent2:
        c.wait_send()
    peers(i, NI, lambda p: z_copy(3, p, p, p).wait_send())
    sib.wait_send()
    peers(t, NT, lambda p: at_copy(p, p, p).wait_send())
    peers(t, NT, lambda p: c1(p, p, p).wait_send())
    peers(t, NT, lambda p: c2(p, p).wait_send())


def local(
    hidden_in,
    norm_gain,
    query_weight,
    w_key,
    value_weight,
    w_output,
    paired_down_matrices,
    query_up_matrices,
    value_up_matrices,
    output_down_matrices,
    output_up_matrices,
    key_cache,
    value_cache,
    cache_lengths,
    row_adapter,
    old_slot,
    new_slot,
):
    smem = pl.BlockSpec(memory_space=pltpu.SMEM)
    vmem = pl.BlockSpec(memory_space=pltpu.VMEM)
    hbm = pl.BlockSpec(memory_space=pl.ANY)
    return pl.pallas_call(
        kernel,
        out_shape=jax.ShapeDtypeStruct((2, ROWS, SH), BF16),
        in_specs=[smem] + [vmem] * 4 + [hbm] * 12,
        out_specs=vmem,
        scratch_shapes=[pltpu.SMEM((8, 128), jnp.int32)]
        + [pltpu.VMEM(*s) for s in SCRATCH.values()]
        + [pltpu.SemaphoreType.DMA(s) for s in SEMS.values()],
        compiler_params=pltpu.CompilerParams(
            collective_id=0, has_side_effects=True, vmem_limit_bytes=58 * 2**20
        ),
        name="decode_block",
    )(
        cache_lengths,
        norm_gain.reshape(4, 128),
        row_adapter.reshape(1, ROWS),
        old_slot.reshape(1, -1),
        new_slot.reshape(1, -1),
        hidden_in,
        query_weight,
        w_key.T,
        value_weight.T,
        w_output,
        paired_down_matrices,
        query_up_matrices,
        jnp.swapaxes(value_up_matrices, 1, 2),
        output_down_matrices,
        output_up_matrices,
        key_cache,
        value_cache,
    )


def solution(mesh):
    placed = (
        P(None, "inst", "tp"),
        P("tp"),
        P(None, "tp"),
        P(None, "tp"),
        P(None, "tp"),
        P("tp", None),
        P("inst", "tp", None),
        P("inst", None, "tp"),
        P("inst", None, "tp"),
        P("inst", None, "tp"),
        P("inst", None, "tp"),
        P(("inst", "tp"), None, None),
        P(("inst", "tp"), None, None),
        P(("inst", "tp")),
        P("inst"),
        P(),
        P(),
    )
    return jax.shard_map(
        local, mesh=mesh, in_specs=placed, out_specs=P(None, "inst", "tp"), check_vma=False
    )
```
